512 devices in a mesh: pts: 16 (over y, core), dir: 16 (over x, z_hi), freq: 2 (over z_lo).
Axes of the slice: x: 4, y: 8, z: 8 (z_hi: 4, z_lo: 2; z = z_hi * 2 + z_lo), core: 2. Of those that a mesh axis runs over, the one named last changes fastest.
Arguments:
- action: float32 [48, 64, 65536], P('freq', 'dir', 'pts'), may hold values from 0.05 to 2
- bathymetry: float32 [65536], P('pts'), may hold values from 20 to 60
- refraction: float32 [48, 65536], P('freq', 'pts'), may hold values from 0.5 to 2
- shifting: float32 [48, 65536], P('freq', 'pts'), may hold values from 0.5 to 2
- heading: float32 [65536], P('pts'), may hold values from -3.140625 to 3.140625
- slope_angle: float32 [65536], P('pts'), may hold values from -3.140625 to 3.140625
- wet_mask: int32 [65536], P('pts'), may hold values 0 or 1
- substeps: int32 [128], P('pts'), may hold values from 1 to 4
Outputs:
- evolved: float32 [48, 64, 65536], P('freq', 'dir', 'pts')
The draws below stay inside these ranges and needn't reach their ends.
All inputs are finite; a program needn't handle non-finite values. Where the reference program divides by a largest or mean magnitude, that divisor is 1e-20 or more. No bound on the sum of `wet_mask` on one device may be relied on, other than what follows from the above.
Results may differ from the reference program's by a relative error of at most 0.00002.
Values sent between devices are 32-bit elements; how exact they have to be, the bound alone decides.
No kernel may reach another device: no remote copies, remote signals or barrier semaphores. Data moves between devices by JAX's collectives and lax.ppermute only.
A program may use at most 64 MiB of HBM per device.

```python
import math
import jax
import jax.numpy as jnp
from jax import lax

FREQ = 48
DIR = 64
KMAX = 4
BLK = 512
P_DEV = 4096
PTS = 65536
NBLK = 128
N_PTS = 16


def place_ends(array, own_key, low, high):
    dims = array.shape
    spot = [jax.random.randint(jax.random.fold_in(own_key, axis), (), 0, dims[axis]) for axis in range(len(dims))]
    array = array.at[tuple(spot)].set(low)
    longest = dims.index(max(dims))
    spot[longest] = (spot[longest] + 1) % dims[longest]
    return array.at[tuple(spot)].set(high)


def block_scale(rng, dims, shards, least, high):
    def one(dim, parts):
        draws = jax.random.uniform(jax.random.fold_in(jax.random.fold_in(rng, 6), dim), (parts,), jnp.float32, least / len(shards), high / len(shards))
        return jnp.repeat(jnp.exp(draws), dims[dim] // parts).reshape((-1,) + (1,) * (len(dims) - dim - 1))

    gain = one(*shards[0])
    for cut in shards[1:]:
        gain = gain * one(*cut)
    return gain


def setup_inputs(seed: int = 0) -> dict:
    streams_of = jax.random.split(jax.random.key(seed), 9)
    action = jnp.clip(jnp.exp(math.log(2.0) - 3.6888794 * jax.random.uniform(streams_of[0], (FREQ, DIR, PTS), jnp.float32) ** block_scale(streams_of[0], (FREQ, DIR, PTS), ((0, 2), (1, 16), (2, 16)), -0.2, 0.2)), 0.05, 2.0)
    bathymetry = jnp.clip(20.0 + 40.0 * jax.random.uniform(streams_of[1], (PTS,), jnp.float32) ** block_scale(streams_of[1], (PTS,), ((0, 16),), -0.2, 0.2), 20.0, 60.0)
    refraction = jnp.clip(jnp.exp(math.log(2.0) - 1.3862944 * jax.random.uniform(streams_of[2], (FREQ, PTS), jnp.float32) ** block_scale(streams_of[2], (FREQ, PTS), ((0, 2), (1, 16)), -0.2, 0.2)), 0.5, 2.0)
    shifting = jnp.clip(jnp.exp(math.log(2.0) - 1.3862944 * jax.random.uniform(streams_of[3], (FREQ, PTS), jnp.float32) ** block_scale(streams_of[3], (FREQ, PTS), ((0, 2), (1, 16)), -0.2, 0.2)), 0.5, 2.0)
    heading = jnp.clip(jax.random.uniform(streams_of[4], (PTS,), jnp.float32, -3.140625, 3.140625), -3.140625, 3.140625)
    slope_angle = jnp.clip(jax.random.uniform(streams_of[5], (PTS,), jnp.float32, -3.140625, 3.140625), -3.140625, 3.140625)
    wet_mask = place_ends((jax.random.randint(streams_of[6], (PTS,), 0, 4) < 3).astype(jnp.int32), jax.random.fold_in(streams_of[6], 1), 0, 1)
    substeps = place_ends(jax.random.randint(streams_of[7], (NBLK,), 1, KMAX + 1), jax.random.fold_in(streams_of[7], 1), 1, KMAX).astype(jnp.int32)
    return dict(action=action, bathymetry=bathymetry, refraction=refraction, shifting=shifting, heading=heading, slope_angle=slope_angle, wet_mask=wet_mask, substeps=substeps)


EPSILON = 1e-6


def sweep(values, courant, weight, active, along):
    extent = values.shape[along]
    lower_cells = lax.slice_in_dim(values, 0, extent - 1, axis=along)
    upper_cells = lax.slice_in_dim(values, 1, extent, axis=along)
    interface = 0.5 * (lax.slice_in_dim(courant, 0, extent - 1, axis=along) + lax.slice_in_dim(courant, 1, extent, axis=along)) * weight
    fluxes = jnp.maximum(interface, 0.0) * lower_cells + jnp.minimum(interface, 0.0) * upper_cells
    change = lax.slice_in_dim(fluxes, 1, extent - 1, axis=along) - lax.slice_in_dim(fluxes, 0, extent - 2, axis=along)
    inner_cells = lax.slice_in_dim(values, 1, extent - 1, axis=along)
    return jnp.where(active, inner_cells - change, inner_cells)


def direction_angles(index):
    return (index.astype(jnp.float32) + 0.5) * (2.0 * math.pi / DIR)


def reference(action, bathymetry, refraction, shifting, heading, slope_angle, wet_mask, substeps):
    padded = jnp.concatenate([bathymetry[:1], bathymetry, bathymetry[-1:]])
    gradient = (padded[2:] - padded[:-2]) * 0.5
    wet_float = wet_mask.astype(jnp.float32)
    turn_base = refraction * gradient[None, :] * wet_float[None, :]
    shift_base = shifting * wet_float[None, :]
    angles = direction_angles(jnp.arange(DIR, dtype=jnp.int32))
    cos_peak = jnp.max(jnp.abs(jnp.cos(angles[:, None] - heading[None, :])), axis=0)
    sin_peak = jnp.max(jnp.abs(jnp.sin(angles[:, None] - slope_angle[None, :])), axis=0)
    peak_turn = jnp.max(jnp.abs(turn_base) * sin_peak[None, :])
    peak_shift = jnp.max(jnp.abs(shift_base) * cos_peak[None, :])
    scale_turn = 0.5 / (peak_turn + EPSILON)
    scale_shift = 0.5 / (peak_shift + EPSILON)
    point_counts = jnp.repeat(substeps, BLK)
    marks = jnp.arange(FREQ + 1, dtype=jnp.int32)
    freq_weight = jnp.where((marks >= 1) & (marks <= FREQ - 1), 1.0, 0.0).astype(jnp.float32)[:, None, None]

    def one_group(group_index, output):
        start = (group_index * P_DEV).astype(jnp.int32)
        spectrum = lax.dynamic_slice_in_dim(action, start, P_DEV, 2)
        turn_part = lax.dynamic_slice_in_dim(turn_base, start, P_DEV, 1)
        shift_part = lax.dynamic_slice_in_dim(shift_base, start, P_DEV, 1)
        heading_part = lax.dynamic_slice_in_dim(heading, start, P_DEV, 0)
        slope_part = lax.dynamic_slice_in_dim(slope_angle, start, P_DEV, 0)
        wet_part = lax.dynamic_slice_in_dim(wet_float, start, P_DEV, 0)
        count_part = lax.dynamic_slice_in_dim(point_counts, start, P_DEV, 0)
        count_float = count_part.astype(jnp.float32)
        sines = jnp.sin(angles[:, None] - slope_part[None, :])
        c_turn = turn_part[:, None, :] * sines[None, :, :]
        courant_turn = c_turn * scale_turn / count_float[None, None, :]
        courant_wrap = jnp.concatenate([courant_turn[:, -1:], courant_turn, courant_turn[:, :1]], axis=1)
        for sweep_index in range(KMAX):
            active = (sweep_index < count_part)[None, None, :]
            wrapped = jnp.concatenate([spectrum[:, -1:], spectrum, spectrum[:, :1]], axis=1)
            spectrum = sweep(wrapped, courant_wrap, 1.0, active, 1)
        cosines = jnp.cos(angles[:, None] - heading_part[None, :])
        c_shift = shift_part[:, None, :] * cosines[None, :, :]
        courant_shift = c_shift * scale_shift / count_float[None, None, :]
        courant_chain = jnp.pad(courant_shift, ((1, 1), (0, 0), (0, 0)))
        for sweep_index in range(KMAX):
            active = (sweep_index < count_part)[None, None, :]
            chained = jnp.pad(spectrum, ((1, 1), (0, 0), (0, 0)))
            spectrum = sweep(chained, courant_chain, freq_weight, active, 0)
        return lax.dynamic_update_slice_in_dim(output, spectrum * wet_part[None, None, :], start, 2)

    return lax.fori_loop(0, N_PTS, one_group, jnp.zeros_like(action))
```

```python
import functools
import math

import jax
import jax.numpy as jnp
import numpy as np
from jax import lax
from jax.experimental import pallas as pl
from jax.experimental.pallas import tpu as pltpu
from jax.sharding import Mesh
from jax.sharding import PartitionSpec as P

FREQ = 48
DIR = 64
KMAX = 4
BLK = 512
SLOTS = 256
EPSILON = 1e-06
LANES = 128
F_LOC = 24
D_LOC = 4
TILES = 32
ROWS = TILES * D_LOC
VMEM_LIMIT = 24 * 1024 * 1024

f32, bf16, i32 = jnp.float32, jnp.bfloat16, jnp.int32


def angle_table():
    step = 2.0 * math.pi / DIR
    half = np.arange(DIR // 2) * step
    centre = (np.arange(DIR // 2) + 0.5) * step
    parts = [np.sin(half), np.cos(half), np.sin(centre), np.cos(centre)]
    return np.concatenate([np.concatenate([p, -p]) for p in parts]).astype(np.float32)


SIN_FACE, COS_FACE, SIN_CELL, COS_CELL = 0, DIR, 2 * DIR, 3 * DIR
COS_HALF = math.cos(math.pi / DIR)


def iota(shape, dim):
    return lax.broadcasted_iota(i32, shape, dim)


def shifted(bath):
    lane = iota((TILES, LANES), 1)
    left = pltpu.roll(bath, 1, 1)
    left = jnp.where(lane == 0, pltpu.roll(left, 1, 0), left)
    right = pltpu.roll(bath, LANES - 1, 1)
    right = jnp.where(lane == LANES - 1, pltpu.roll(right, TILES - 1, 0), right)
    return left, right


def end_points():
    point = iota((TILES, LANES), 0) * LANES + iota((TILES, LANES), 1)
    return point == 0, point == TILES * LANES - 1


def full_gradient(meta, bath, below, above):
    left, right = shifted(bath)
    first, last = end_points()
    from_below, _ = shifted(below)
    _, from_above = shifted(above)
    lo = jnp.where(meta[2] == 0, bath, from_below)
    hi = jnp.where(meta[2] == 15, bath, from_above)
    return (jnp.where(last, hi, right) - jnp.where(first, lo, left)) * 0.5


def face_sine(table, face, sin_s, cos_s):
    at = lax.rem(face + DIR, DIR)
    return table[SIN_FACE + at] * cos_s - table[COS_FACE + at] * sin_s


def masks(table, meta, bath, slope, wet):
    left, right = shifted(bath)
    drive = (right - left) * wet
    first, last = end_points()
    ends = first | last
    sin_s, cos_s = jnp.sin(slope), jnp.cos(slope)

    def at(face):
        speed = drive * face_sine(table, face, sin_s, cos_s)
        return (speed > 0.0) | ends, (speed < 0.0) | ends

    return at


def ranks(mask):
    on = jnp.where(mask, 1.0, 0.0).astype(f32)
    row, col = iota((LANES, LANES), 0), iota((LANES, LANES), 1)
    before = jnp.where(row < col, 1.0, 0.0).astype(bf16)
    ones = jnp.ones((LANES, LANES), bf16)
    r, c = iota((TILES, TILES), 0), iota((TILES, TILES), 1)
    earlier = jnp.where((c < r) & (r // 4 == c // 4), 1.0, 0.0).astype(bf16)
    inner = jnp.dot(on.astype(bf16), before, preferred_element_type=f32)
    outer = jnp.dot(earlier, on.astype(bf16), preferred_element_type=f32)
    outer = jnp.dot(outer.astype(bf16), ones, preferred_element_type=f32)
    return jnp.where(mask, inner + outer, -1.0)


def selector(rank_ref, block, wave):
    slot = (iota((SLOTS, LANES), 0) + wave * SLOTS).astype(f32)
    parts = [
        jnp.where(rank_ref[pl.ds(4 * block + j, 1), :] == slot, 1.0, 0.0).astype(f32) for j in range(4)
    ]
    return jnp.concatenate(parts, axis=1).astype(bf16)


def in_three(x):
    high = x.astype(bf16)
    rest = x - high.astype(f32)
    mid = rest.astype(bf16)
    low = (rest - mid.astype(f32)).astype(bf16)
    return jnp.concatenate([high, mid, low], axis=0)


def add_three(y, rows):
    return (y[:rows] + y[rows : 2 * rows]) + y[2 * rows :]


def pack_kernel(wave, meta, table, x_ref, bath_ref, slope_ref, wet_ref, up_ref, down_ref, up_rank, down_rank):
    at = masks(table, meta, bath_ref[...], slope_ref[...], wet_ref[...].astype(f32))
    up_rank[...] = ranks(at(D_LOC * meta[0] + D_LOC)[0])
    down_rank[...] = ranks(at(D_LOC * meta[0])[1])
    rows = D_LOC * F_LOC

    def one(block, carry):
        cells = []
        for j in range(4):
            cells.append(
                jnp.concatenate(
                    [x_ref[pl.ds((4 * block + j) * D_LOC + d, F_LOC, stride=ROWS), :] for d in range(D_LOC)],
                    axis=0,
                )
            )
        parts = in_three(jnp.concatenate(cells, axis=1))
        for rank_ref, out_ref in ((up_rank, up_ref), (down_rank, down_ref)):
            chosen = lax.dot_general(
                parts,
                selector(rank_ref, block, wave),
                (((1,), (1,)), ((), ())),
                preferred_element_type=f32,
            )
            out_ref[:, pl.ds(pl.multiple_of(block * SLOTS, SLOTS), SLOTS)] = add_three(chosen, rows)
        return carry

    lax.fori_loop(0, 8, one, 0)


def peak_kernel(meta, table, bath_ref, below_ref, above_ref, slope_ref, heading_ref, wet_ref, refr_ref, shift_ref, out, turn_row, shift_row, marks):
    wet = wet_ref[...].astype(f32)
    gradient = full_gradient(meta, bath_ref[...], below_ref[...], above_ref[...])
    slope, heading = slope_ref[...], heading_ref[...]
    sin_s, cos_s, sin_h, cos_h = jnp.sin(slope), jnp.cos(slope), jnp.sin(heading), jnp.cos(heading)
    sin_peak = jnp.zeros((TILES, LANES), f32)
    cos_peak = jnp.zeros((TILES, LANES), f32)
    for d in range(DIR // 2):
        sin_a, cos_a = table[SIN_CELL + d], table[COS_CELL + d]
        sin_peak = jnp.maximum(sin_peak, jnp.abs(sin_a * cos_s - cos_a * sin_s))
        cos_peak = jnp.maximum(cos_peak, jnp.abs(cos_a * cos_h + sin_a * sin_h))
    turn_row[...] = jnp.abs(gradient) * wet * sin_peak
    shift_row[...] = wet * cos_peak
    turn = jnp.zeros((8, LANES), f32)
    shift = jnp.zeros((8, LANES), f32)
    for t in range(TILES):
        coef, shift_coef = turn_row[t : t + 1, :], shift_row[t : t + 1, :]
        for k in range(3):
            rows = slice(k * 256 + t * 8, k * 256 + t * 8 + 8)
            turn = jnp.maximum(turn, jnp.abs(refr_ref[rows, :]) * coef)
            shift = jnp.maximum(shift, jnp.abs(shift_ref[rows, :]) * shift_coef)
    at = masks(table, meta, bath_ref[...], slope, wet)
    for i in range(8):
        low, high = at(D_LOC * i)
        marks[2 * i * TILES : (2 * i + 1) * TILES, :] = jnp.where(low, 1.0, 0.0).astype(f32)
        marks[(2 * i + 1) * TILES : (2 * i + 2) * TILES, :] = jnp.where(high, 1.0, 0.0).astype(f32)
    ones = jnp.ones((LANES, LANES), bf16)
    group = jnp.where(iota((LANES, 4 * LANES), 0) == iota((LANES, 4 * LANES), 1) // 4, 1.0, 0.0).astype(bf16)
    per_block = jnp.dot(group, marks[...].astype(bf16), preferred_element_type=f32)
    per_block = jnp.dot(per_block.astype(bf16), ones, preferred_element_type=f32)
    out[0] = jnp.max(turn)
    out[1] = jnp.max(shift)
    out[2] = jnp.max(per_block)
    out[3] = 0.0


def turn_kernel(edge, meta, table, peaks, count, x_ref, bath_ref, below_ref, above_ref, slope_ref, wet_ref, refr_ref, left_ref, right_ref, left_more, right_more, *rest):
    if edge:
        y_ref, rim_ref, low_rank, high_rank, speed, sines, halo_l, halo_r = rest
    else:
        y_ref, low_rank, high_rank, speed, sines, halo_l, halo_r = rest
    wet = wet_ref[...].astype(f32)
    at = masks(table, meta, bath_ref[...], slope_ref[...], wet)
    low_rank[...] = ranks(at(D_LOC * meta[0])[0])
    high_rank[...] = ranks(at(D_LOC * meta[0] + D_LOC)[1])
    scale = 0.5 / (jnp.full((TILES, LANES), peaks[0], f32) + EPSILON)
    gradient = full_gradient(meta, bath_ref[...], below_ref[...], above_ref[...])
    tile_block = iota((TILES, LANES), 0) // 4
    counts = jnp.zeros((TILES, LANES), i32)
    for b in range(8):
        counts = jnp.where(tile_block == b, count[b], counts)
    speed[...] = gradient * wet * scale * COS_HALF / counts.astype(f32)
    slope = slope_ref[...]
    sin_s, cos_s = jnp.sin(slope), jnp.cos(slope)
    faces = D_LOC + 2 * KMAX - 1
    for k in range(faces):
        sines[k * TILES : (k + 1) * TILES, :] = face_sine(table, D_LOC * meta[0] - KMAX + 1 + k, sin_s, cos_s)
    first = 2 * (1 - meta[1]) if edge else meta[1]
    groups = 1 if edge else 2
    rows = D_LOC * groups * 8
    overflow = peaks[2] > SLOTS

    def one(block, carry):
        columns = pl.ds(pl.multiple_of(block * SLOTS, SLOTS), SLOTS)

        def sent(ref):
            return in_three(
                jnp.concatenate(
                    [
                        ref[pl.ds(pl.multiple_of(d * F_LOC + first * 8, 8), groups * 8), columns]
                        for d in range(D_LOC)
                    ],
                    axis=0,
                )
            )

        for rank_ref, ref, more, halo in (
            (low_rank, left_ref, left_more, halo_l),
            (high_rank, right_ref, right_more, halo_r),
        ):
            halo[...] = add_three(
                jnp.dot(sent(ref), selector(rank_ref, block, 0), preferred_element_type=f32), rows
            )

            @pl.when(overflow)
            def _():
                halo[...] += add_three(
                    jnp.dot(sent(more), selector(rank_ref, block, 1), preferred_element_type=f32), rows
                )

        steps = count[block]
        for kmax in range(1, KMAX + 1):

            @pl.when(steps == kmax)
            def _():
                for j in range(4):
                    tile = 4 * block + j
                    lanes = slice(j * LANES, (j + 1) * LANES)
                    drive = speed[pl.ds(tile, 1), :]
                    sine = {
                        k: sines[pl.ds(k * TILES + tile, 1), :]
                        for k in range(KMAX - kmax, faces - (KMAX - kmax))
                    }
                    for g in range(groups):
                        group = first + g
                        base = refr_ref[pl.ds(pl.multiple_of(group * 256 + tile * 8, 8), 8), :] * drive
                        cells = []
                        for c in range(KMAX - kmax, D_LOC + KMAX + kmax):
                            d = c % D_LOC
                            at_row = d * groups * 8 + g * 8
                            if c < KMAX:
                                cells.append(halo_l[at_row : at_row + 8, lanes])
                            elif c < KMAX + D_LOC:
                                cells.append(x_ref[pl.ds(group * 8 * ROWS + tile * D_LOC + d, 8, stride=ROWS), :])
                            else:
                                cells.append(halo_r[at_row : at_row + 8, lanes])
                        face = [base * sine[k] for k in sorted(sine)]
                        plus = [jnp.maximum(v, 0.0) for v in face]
                        minus = [jnp.minimum(v, 0.0) for v in face]
                        for step in range(kmax):
                            n = len(cells) - 1
                            flux = [
                                plus[step + i] * cells[i] + minus[step + i] * cells[i + 1] for i in range(n)
                            ]
                            cells = [cells[i + 1] - (flux[i + 1] - flux[i]) for i in range(n - 1)]
                        for d in range(D_LOC):
                            y_ref[pl.ds(g * 8 * ROWS + tile * D_LOC + d, 8, stride=ROWS), :] = cells[d]

        return carry

    lax.fori_loop(0, 8, one, 0)
    if edge:
        for m in range(KMAX):
            row = jnp.where(meta[1] == 0, 7 - m, m)
            rim_ref[m * ROWS : (m + 1) * ROWS, :] = y_ref[pl.ds(pl.multiple_of(row * ROWS, ROWS), ROWS), :]


def shift_kernel(meta, table, peaks, count, near_ref, far_ref, rim_ref, shift_ref, shift_rim_ref, heading_ref, wet_ref, out_ref, sines, cosines, speed):
    wet = wet_ref[...].astype(f32)
    scale = 0.5 / (jnp.full((TILES, LANES), peaks[1], f32) + EPSILON)
    tile_block = iota((TILES, LANES), 0) // 4
    counts = jnp.zeros((TILES, LANES), i32)
    for b in range(8):
        counts = jnp.where(tile_block == b, count[b], counts)
    heading = heading_ref[...]
    sines[...] = jnp.sin(heading)
    cosines[...] = jnp.cos(heading)
    lower = meta[1] == 0
    sign = jnp.where(lower, 0.5, -0.5)
    speed[...] = wet * scale * sign / counts.astype(f32)
    row = iota((8, LANES), 0)
    sin_a = jnp.zeros((8, LANES), f32)
    cos_a = jnp.zeros((8, LANES), f32)
    for d in range(D_LOC):
        here = row % D_LOC == d
        sin_a = jnp.where(here, table[SIN_CELL + D_LOC * meta[0] + d], sin_a)
        cos_a = jnp.where(here, table[COS_CELL + D_LOC * meta[0] + d], cos_a)
    upper_rows = row < D_LOC

    def spread(ref, first, second):
        return jnp.where(upper_rows, ref[pl.ds(first, 1), :], ref[pl.ds(second, 1), :])

    def one(pair, carry):
        tile = 2 * pair
        offset = pl.multiple_of(pair * 8, 8)
        wave = cos_a * spread(cosines, tile, tile + 1) + sin_a * spread(sines, tile, tile + 1)
        drive = wave * spread(speed, tile, tile + 1)
        forward = drive > 0.0
        mask_wet = spread_wet(pair)

        def freq(g):
            return jnp.where(lower, g, F_LOC - 1 - g)

        def coefficient(g):
            f = freq(g)
            at = (f // 8) * 256 + lax.rem(f, 8)
            return spread(shift_ref, at + tile * 8, at + tile * 8 + 8)

        def rim_coefficient(m):
            at = jnp.where(lower, m, 7 - m)
            return spread(shift_rim_ref, at + tile * 8, at + tile * 8 + 8)

        steps = count[pair // 2]
        for kmax in range(1, KMAX + 1):

            @pl.when(steps == kmax)
            def _():
                cells, coefs = [], []
                for g in range(F_LOC):
                    coefs.append(coefficient(g))
                    if g < 16:
                        at = jnp.where(lower, g, 15 - g)
                        cells.append(far_ref[pl.ds(pl.multiple_of(at * ROWS + offset, 8), 8), :])
                    else:
                        at = jnp.where(lower, g - 16, 23 - g)
                        cells.append(near_ref[pl.ds(pl.multiple_of(at * ROWS + offset, 8), 8), :])
                for m in range(kmax):
                    coefs.append(rim_coefficient(m))
                    cells.append(rim_ref[pl.ds(pl.multiple_of(m * ROWS + offset, 8), 8), :])
                face = [(coefs[i] + coefs[i + 1]) * drive for i in range(len(coefs) - 1)]
                for _step in range(kmax):
                    n = len(cells)
                    flux = [face[i] * jnp.where(forward, cells[i], cells[i + 1]) for i in range(n - 1)]
                    cells = [cells[0] - flux[0]] + [cells[i] - (flux[i] - flux[i - 1]) for i in range(1, n - 1)]
                for g in range(F_LOC):
                    out_ref[pl.ds(pl.multiple_of(freq(g) * ROWS + offset, 8), 8), :] = cells[g] * mask_wet

        return carry

    def spread_wet(pair):
        return spread(wets, 2 * pair, 2 * pair + 1)

    wets = Wet(wet_ref)
    lax.fori_loop(0, TILES // 2, one, 0)


class Wet:
    def __init__(self, ref):
        self.ref = ref

    def __getitem__(self, index):
        return self.ref[index].astype(f32)


SMEM = pl.BlockSpec(memory_space=pltpu.SMEM)
VMEM = pl.BlockSpec(memory_space=pltpu.VMEM)


def call(body, outs, in_specs, scratch, flops, moved, args, out_specs=None):
    return pl.pallas_call(
        body,
        out_shape=outs,
        in_specs=in_specs,
        out_specs=out_specs if out_specs is not None else [VMEM] * len(outs),
        scratch_shapes=scratch,
        compiler_params=pltpu.CompilerParams(vmem_limit_bytes=VMEM_LIMIT),
        cost_estimate=pl.CostEstimate(flops=flops, bytes_accessed=moved, transcendentals=0),
    )(*args)


def shape(*dims):
    return jax.ShapeDtypeStruct(dims, f32)


def local(action, bathymetry, refraction, shifting, heading, slope_angle, wet_mask, substeps):
    pts = lax.axis_index(("pts_0", "pts_1"))
    dir_index, freq_index = lax.axis_index("dir"), lax.axis_index("freq")
    meta = jnp.stack([dir_index, freq_index, pts, pts]).astype(i32)
    table = jnp.asarray(angle_table())
    x = action.reshape(F_LOC, D_LOC, TILES, LANES).transpose(0, 2, 1, 3).reshape(F_LOC * ROWS, LANES)
    bath, head, slope, wet = (
        a.reshape(TILES, LANES) for a in (bathymetry, heading, slope_angle, wet_mask)
    )

    def by_eight(a):
        return a.reshape(3, 8, TILES, LANES).transpose(0, 2, 1, 3).reshape(3 * TILES * 8, LANES)

    refr, shift = by_eight(refraction), by_eight(shifting)

    def ring(axis, by):
        count = lax.axis_size(axis)
        return [(i, (i + by) % count) for i in range(count)]

    pts_axes = ("pts_0", "pts_1")
    below = lax.ppermute(bath, pts_axes, ring(pts_axes, 1))
    above = lax.ppermute(bath, pts_axes, ring(pts_axes, -1))

    packed = [shape(D_LOC * F_LOC, 8 * SLOTS)] * 2
    rank = pltpu.VMEM((TILES, LANES), f32)

    def exchange(wave):
        up, down = call(
            functools.partial(pack_kernel, wave),
            packed,
            [SMEM, SMEM] + [VMEM] * 4,
            [rank, rank],
            10**9,
            4 * 10**6,
            (meta, table, x, bath, slope, wet),
        )
        return lax.ppermute(up, "dir", ring("dir", 1)), lax.ppermute(down, "dir", ring("dir", -1))

    left, right = exchange(0)

    rim_group = lax.dynamic_slice(shift, (2 * (1 - freq_index) * 256, 0), (256, LANES))
    swap = [(0, 1), (1, 0)]
    shift_rim = lax.ppermute(rim_group, "freq", swap)

    (local_peaks,) = call(
        peak_kernel,
        [shape(4)],
        [SMEM, SMEM] + [VMEM] * 8,
        [rank, rank, pltpu.VMEM((16 * TILES, LANES), f32)],
        10**7,
        10**6,
        (meta, table, bath, below, above, slope, head, wet, refr, shift),
        out_specs=[SMEM],
    )
    peaks = local_peaks
    for axis in ("pts_0", "pts_1", "freq"):
        peaks = lax.pmax(peaks, axis)

    left_more, right_more = lax.cond(
        peaks[2] > SLOTS,
        lambda: exchange(1),
        lambda: (jnp.zeros((D_LOC * F_LOC, 8 * SLOTS), f32), jnp.zeros((D_LOC * F_LOC, 8 * SLOTS), f32)),
    )

    def turn(edge):
        groups = 1 if edge else 2
        outs = [shape(groups * 8 * ROWS, LANES)] + ([shape(KMAX * ROWS, LANES)] if edge else [])
        halo = pltpu.VMEM((D_LOC * groups * 8, BLK), f32)
        return call(
            functools.partial(turn_kernel, edge),
            outs,
            [SMEM] * 4 + [VMEM] * 11,
            [rank, rank, rank, pltpu.VMEM(((D_LOC + 2 * KMAX - 1) * TILES, LANES), f32), halo, halo],
            10**8,
            4 * 10**6,
            (meta, table, peaks, substeps, x, bath, below, above, slope, wet, refr, left, right, left_more, right_more),
        )

    near, rim = turn(True)
    other_rim = lax.ppermute(rim, "freq", swap)
    (far,) = turn(False)
    (out,) = call(
        shift_kernel,
        [shape(F_LOC * ROWS, LANES)],
        [SMEM] * 4 + [VMEM] * 7,
        [rank, rank, rank],
        10**8,
        4 * 10**6,
        (meta, table, peaks, substeps, near, far, other_rim, shift, shift_rim, head, wet),
    )
    return out.reshape(F_LOC, TILES, D_LOC, LANES).transpose(0, 2, 1, 3).reshape(F_LOC, D_LOC, TILES * LANES)


PTS = ("pts_0", "pts_1")


def solution(mesh):
    torus = Mesh(
        mesh.devices.reshape(8, 2, mesh.shape["dir"], mesh.shape["freq"]),
        ("pts_0", "pts_1", "dir", "freq"),
    )
    in_specs = (
        P("freq", "dir", PTS),
        P(PTS),
        P("freq", PTS),
        P("freq", PTS),
        P(PTS),
        P(PTS),
        P(PTS),
        P(PTS),
    )
    return jax.shard_map(local, mesh=torus, in_specs=in_specs, out_specs=P("freq", "dir", PTS), check_vma=False)
```

```python
import functools
import math

import jax
import jax.numpy as jnp
import numpy as np
from jax import lax
from jax.experimental import pallas as pl
from jax.experimental.pallas import tpu as pltpu
from jax.sharding import Mesh
from jax.sharding import PartitionSpec as P

FREQ = 48
DIR = 64
KMAX = 4
BLK = 512
SLOTS = 256
EPSILON = 1e-06
LANES = 128
F_LOC = 24
D_LOC = 4
TILES = 32
ROWS = TILES * D_LOC
VMEM_LIMIT = 24 * 1024 * 1024
LOW = -3.0e38

f32, bf16, i32 = jnp.float32, jnp.bfloat16, jnp.int32


def angle_table():
    step = 2.0 * math.pi / DIR
    half = np.arange(DIR // 2) * step
    centre = (np.arange(DIR // 2) + 0.5) * step
    parts = [np.sin(half), np.cos(half), np.sin(centre), np.cos(centre)]
    return np.concatenate([np.concatenate([p, -p]) for p in parts]).astype(np.float32)


SIN_FACE, COS_FACE, SIN_CELL, COS_CELL = 0, DIR, 2 * DIR, 3 * DIR
COS_HALF = math.cos(math.pi / DIR)
FACES = D_LOC + 2 * KMAX - 1


def iota(shape, dim):
    return lax.broadcasted_iota(i32, shape, dim)


def shifted(bath):
    lane = iota((TILES, LANES), 1)
    left = pltpu.roll(bath, 1, 1)
    left = jnp.where(lane == 0, pltpu.roll(left, 1, 0), left)
    right = pltpu.roll(bath, LANES - 1, 1)
    right = jnp.where(lane == LANES - 1, pltpu.roll(right, TILES - 1, 0), right)
    return left, right


def end_points():
    point = iota((TILES, LANES), 0) * LANES + iota((TILES, LANES), 1)
    return point == 0, point == TILES * LANES - 1


def face_sine(table, face, sin_s, cos_s):
    at = lax.rem(face + DIR, DIR)
    return table[SIN_FACE + at] * cos_s - table[COS_FACE + at] * sin_s


def masks(table, bath, wet, sin_s, cos_s):
    left, right = shifted(bath)
    drive = (right - left) * wet
    first, last = end_points()
    ends = first | last

    def at(face):
        speed = drive * face_sine(table, face, sin_s, cos_s)
        return (speed > 0.0) | ends, (speed < 0.0) | ends

    return at


def ranks(mask):
    on = jnp.where(mask, 1.0, 0.0).astype(f32).astype(bf16)
    row, col = iota((LANES, LANES), 0), iota((LANES, LANES), 1)
    before = jnp.where(row < col, 1.0, 0.0).astype(bf16)
    ones = jnp.ones((LANES, LANES), bf16)
    r, c = iota((TILES, TILES), 0), iota((TILES, TILES), 1)
    earlier = jnp.where((c < r) & (r // 4 == c // 4), 1.0, 0.0).astype(bf16)
    inner = jnp.dot(on, before, preferred_element_type=f32)
    number = jnp.dot(on, ones, preferred_element_type=f32)
    offset = jnp.dot(earlier, on, preferred_element_type=f32)
    offset = jnp.dot(offset.astype(bf16), ones, preferred_element_type=f32)
    return inner.astype(i32), offset.astype(i32), number.astype(i32)


def gather(x, index):
    return jnp.take_along_axis(x, index, axis=1)


def packing(mask, wave, source_ref, slot_ref):
    inner, offset, number = ranks(mask)
    lane = iota((TILES, LANES), 1)
    code = jnp.where(mask, (lane - inner) * 128 + lane + 65536, 0)
    for bit in range(7):
        step = 1 << bit
        far = pltpu.roll(code, LANES - step, 1)
        comes = (far & (128 << bit)) != 0
        goes = (code & (128 << bit)) != 0
        code = jnp.where(comes, far - (128 << bit), jnp.where(goes, 0, code))
    source = gather((code & 127).astype(f32), (lane - offset) & 127)
    source_ref[...] = source.astype(i32)
    slot = lane + ((offset - lane + 127) >> 7) * LANES
    slot_ref[...] = jnp.where(slot < offset + number, slot - wave * SLOTS, -1)


def pack_block(x_ref, block, source, slot, outs):
    for d in range(D_LOC):
        for g in range(3):
            x = [x_ref[pl.ds(g * 8 * ROWS + (4 * block + j) * D_LOC + d, 8, stride=ROWS), :] for j in range(4)]
            for s_ref, k_ref, out in zip(source, slot, outs):
                low = jnp.zeros((8, LANES), f32)
                high = jnp.zeros((8, LANES), f32)
                for j in range(4):
                    tile = pl.ds(4 * block + j, 1)
                    taken = gather(x[j], jnp.broadcast_to(s_ref[tile, :], (8, LANES)))
                    half = jnp.broadcast_to(k_ref[tile, :], (8, LANES)) >> 7
                    low = jnp.where(half == 0, taken, low)
                    high = jnp.where(half == 1, taken, high)
                rows = slice((d * 3 + g) * 8, (d * 3 + g) * 8 + 8)
                out[rows, pl.ds(pl.multiple_of(block * SLOTS, SLOTS), LANES)] = low
                out[rows, pl.ds(pl.multiple_of(block * SLOTS + LANES, LANES), LANES)] = high


def more_kernel(meta, table, x_ref, bath_ref, slope_ref, wet_ref, up_ref, down_ref, *scratch):
    slope = slope_ref[...]
    at = masks(table, bath_ref[...], wet_ref[...].astype(f32), jnp.sin(slope), jnp.cos(slope))
    packing(at(D_LOC * meta[0] + D_LOC)[0], 1, scratch[0], scratch[1])
    packing(at(D_LOC * meta[0])[1], 1, scratch[2], scratch[3])

    def one(block, carry):
        pack_block(x_ref, block, scratch[::2], scratch[1::2], (up_ref, down_ref))
        return carry

    lax.fori_loop(0, 8, one, 0)


def part(edge, meta):
    return (2 * (1 - meta[1]), 1) if edge else (meta[1], 2)


def rows_of(x_hbm, edge, meta):
    first, groups = part(edge, meta)
    return x_hbm.at[pl.ds(pl.multiple_of(first * 8 * ROWS, 8 * ROWS), groups * 8 * ROWS), :]


def fetch(pairs, sems):
    copies = [pltpu.make_async_copy(source, target, sems.at[i]) for i, (source, target) in enumerate(pairs)]
    for copy in copies:
        copy.start()
    return copies


def pack_kernel(meta, table, bath_hbm, slope_hbm, wet_hbm, x_hbm, up_hbm, down_hbm, bath_ref, slope_ref, wet_ref, x_ref, up_ref, down_ref, sems, in_sems, up_sems, down_sems, *scratch):
    def arrival(c):
        rows = pl.ds(pl.multiple_of(c * 8 * D_LOC, 8 * D_LOC), 8 * D_LOC)
        return pltpu.make_async_copy(x_hbm.at[:, rows, :], x_ref.at[:, rows, :], in_sems.at[c])

    def departures(c):
        columns = pl.ds(pl.multiple_of(c * 2 * SLOTS, 2 * SLOTS), 2 * SLOTS)
        return (
            pltpu.make_async_copy(up_ref.at[:, columns], up_hbm.at[:, columns], up_sems.at[c]),
            pltpu.make_async_copy(down_ref.at[:, columns], down_hbm.at[:, columns], down_sems.at[c]),
        )

    copies = fetch(((bath_hbm, bath_ref), (slope_hbm, slope_ref), (wet_hbm, wet_ref)), sems)
    for c in range(4):
        arrival(c).start()
    for copy in copies:
        copy.wait()
    slope = slope_ref[...]
    at = masks(table, bath_ref[...], wet_ref[...].astype(f32), jnp.sin(slope), jnp.cos(slope))
    packing(at(D_LOC * meta[0] + D_LOC)[0], 0, scratch[0], scratch[1])
    packing(at(D_LOC * meta[0])[1], 0, scratch[2], scratch[3])
    flat = x_ref.reshape(F_LOC * ROWS, LANES)

    def two(c, carry):
        arrival(c).wait()
        for block in (2 * c, 2 * c + 1):
            pack_block(flat, block, scratch[::2], scratch[1::2], (up_ref, down_ref))
        for copy in departures(c):
            copy.start()
        return carry

    lax.fori_loop(0, 4, two, 0)
    for c in range(4):
        for copy in departures(c):
            copy.wait()


def note_kernel(meta, table, count, bath_hbm, slope_hbm, wet_hbm, heading_hbm, refr_hbm, shift_hbm, note_ref, halo_ref, sine_ref, wave_ref, shift_rim_ref, bath_ref, slope_ref, wet_ref, heading_ref, refr_ref, shift_ref, sems, turn_row, shift_row, refr_row, marks):
    copies = fetch(
        (
            (bath_hbm, bath_ref),
            (slope_hbm, slope_ref),
            (wet_hbm, wet_ref),
            (heading_hbm, heading_ref),
            (refr_hbm, refr_ref),
            (shift_hbm, shift_ref),
        ),
        sems,
    )
    for copy in copies[:4]:
        copy.wait()
    wet, bath = wet_ref[...].astype(f32), bath_ref[...]
    slope, heading = slope_ref[...], heading_ref[...]
    sin_s, cos_s, sin_h, cos_h = jnp.sin(slope), jnp.cos(slope), jnp.sin(heading), jnp.cos(heading)
    at = masks(table, bath, wet, sin_s, cos_s)
    sin_peak = jnp.zeros((TILES, LANES), f32)
    cos_peak = jnp.zeros((TILES, LANES), f32)
    for d in range(DIR // 2):
        sin_a, cos_a = table[SIN_CELL + d], table[COS_CELL + d]
        sin_peak = jnp.maximum(sin_peak, jnp.abs(sin_a * cos_s - cos_a * sin_s))
        cos_peak = jnp.maximum(cos_peak, jnp.abs(cos_a * cos_h + sin_a * sin_h))
    left, right = shifted(bath)
    first, last = end_points()
    gradient = jnp.where(first | last, 0.0, (right - left) * 0.5)
    turn_row[...] = jnp.abs(gradient) * wet * sin_peak
    shift_row[...] = wet * cos_peak
    turn = jnp.zeros((8, LANES), f32)
    shift = jnp.zeros((8, LANES), f32)
    ends = []
    for copy in copies[4:]:
        copy.wait()
    for t in range(TILES):
        coef, shift_coef = turn_row[t : t + 1, :], shift_row[t : t + 1, :]
        most, most_shift = jnp.zeros((8, LANES), f32), jnp.zeros((8, LANES), f32)
        for k in range(3):
            rows = slice(k * 256 + t * 8, k * 256 + t * 8 + 8)
            most = jnp.maximum(most, jnp.abs(refr_ref[rows, :]))
            most_shift = jnp.maximum(most_shift, jnp.abs(shift_ref[rows, :]))
        turn = jnp.maximum(turn, most * coef)
        shift = jnp.maximum(shift, most_shift * shift_coef)
        if t in (0, TILES - 1):
            ends.append(jnp.max(most, axis=0, keepdims=True))
    for i in range(8):
        low, high = at(D_LOC * i)
        marks[2 * i * TILES : (2 * i + 1) * TILES, :] = jnp.where(low, 1.0, 0.0).astype(f32)
        marks[(2 * i + 1) * TILES : (2 * i + 2) * TILES, :] = jnp.where(high, 1.0, 0.0).astype(f32)
    ones = jnp.ones((LANES, LANES), bf16)
    group = jnp.where(iota((LANES, 4 * LANES), 0) == iota((LANES, 4 * LANES), 1) // 4, 1.0, 0.0).astype(bf16)
    per_block = jnp.dot(group, marks[...].astype(bf16), preferred_element_type=f32)
    per_block = jnp.dot(per_block.astype(bf16), ones, preferred_element_type=f32)

    weight = wet * sin_peak
    row, lane = iota((8, LANES), 0), iota((8, LANES), 1)
    note = jnp.where(row == 0, jnp.where(lane == 0, jnp.max(turn), jnp.max(shift)), LOW)
    note = jnp.where((row == 0) & (lane == 2), jnp.max(per_block), note)
    refr_row[0:1, :] = ends[0] * weight[0:1, :]
    refr_row[1:2, :] = ends[1] * weight[TILES - 1 : TILES, :]
    mine = lane == meta[2]
    for r, value in enumerate(
        (
            bath_ref[0:1, 0:1],
            bath_ref[0:1, 1:2],
            bath_ref[TILES - 1 : TILES, LANES - 2 : LANES - 1],
            bath_ref[TILES - 1 : TILES, LANES - 1 : LANES],
            refr_row[0:1, 0:1],
            refr_row[1:2, LANES - 1 : LANES],
        )
    ):
        note = jnp.where((row == 1 + r) & mine, value, note)
    note_ref[...] = note
    first = 2 * (1 - meta[1])
    for m in range(KMAX):
        row = jnp.where(meta[1] == 0, 7 - m, m)
        shift_rim_ref[m * TILES : (m + 1) * TILES, :] = shift_ref[pl.ds(first * 256 + row, TILES, stride=8), :]

    unpacking(at(D_LOC * meta[0])[0], halo_ref, 0)
    unpacking(at(D_LOC * meta[0] + D_LOC)[1], halo_ref, 2)
    for k in range(FACES):
        sine_ref[k * TILES : (k + 1) * TILES, :] = face_sine(table, D_LOC * meta[0] - KMAX + 1 + k, sin_s, cos_s)
    sign = jnp.where(meta[1] == 0, 0.5, -0.5)
    speed = wet * sign / block_counts(count)
    for d in range(D_LOC):
        sin_a, cos_a = table[SIN_CELL + D_LOC * meta[0] + d], table[COS_CELL + D_LOC * meta[0] + d]
        wave_ref[pl.ds(d, TILES, stride=D_LOC), :] = (cos_a * cos_h + sin_a * sin_h) * speed


def full_gradient(meta, note, bath):
    row, lane = iota((8, LANES), 0), iota((8, LANES), 1)
    below = jnp.max(jnp.where((row == 4) & (lane == meta[2] - 1), note, LOW))
    above = jnp.max(jnp.where((row == 1) & (lane == meta[2] + 1), note, LOW))
    left, right = shifted(bath)
    first, last = end_points()
    left = jnp.where(first, jnp.where(meta[2] == 0, bath, below), left)
    right = jnp.where(last, jnp.where(meta[2] == 15, bath, above), right)
    return (right - left) * 0.5


def largest_turn(note):
    lane = iota((1, LANES), 1)
    first, second, second_last, last = (note[r : r + 1, :] for r in range(1, 5))
    below = jnp.where(lane == 0, first, pltpu.roll(jnp.broadcast_to(last, (8, LANES)), 1, 1)[0:1, :])
    above = jnp.where(lane == 15, last, pltpu.roll(jnp.broadcast_to(first, (8, LANES)), LANES - 1, 1)[0:1, :])
    at_first = jnp.abs(second - below) * 0.5 * note[5:6, :]
    at_last = jnp.abs(above - second_last) * 0.5 * note[6:7, :]
    here = jnp.where(lane < 16, jnp.maximum(at_first, at_last), 0.0)
    return jnp.maximum(jnp.max(here), jnp.max(jnp.where(lane == 0, note[0:1, :], 0.0)))


def block_counts(count):
    tile_block = iota((TILES, LANES), 0) // 4
    counts = jnp.zeros((TILES, LANES), i32)
    for b in range(8):
        counts = jnp.where(tile_block == b, count[b], counts)
    return counts.astype(f32)


def unpacking(mask, ref, at):
    inner, offset, _ = ranks(mask)
    ref[at * TILES : (at + 1) * TILES, :] = (inner + offset) & 127
    ref[(at + 1) * TILES : (at + 2) * TILES, :] = (offset - iota((TILES, LANES), 1) + 127) >> 7


def turn_kernel(edge, meta, count, note_ref, other_ref, x_hbm, bath_ref, wet_ref, refr_ref, halo_ref, sines, left_ref, right_ref, left_hbm, right_hbm, *rest):
    if edge:
        y_ref, rim_ref, *rest = rest
    else:
        y_ref, *rest = rest
    speed, left_more, right_more, x_ref, sems = rest
    (copy,) = fetch(((rows_of(x_hbm, edge, meta), x_ref),), sems)
    note = jnp.maximum(note_ref[...], other_ref[0:8, :])
    scale = 0.5 / (jnp.full((TILES, LANES), largest_turn(note), f32) + EPSILON)
    wet = wet_ref[...].astype(f32)
    speed[...] = full_gradient(meta, note, bath_ref[...]) * wet * scale * COS_HALF / block_counts(count)
    first, groups = part(edge, meta)
    copy.wait()
    overflow = jnp.max(jnp.where(iota((1, LANES), 1) == 2, note[0:1, :], LOW)) > SLOTS

    def halo(wide, d, g, block, refs, tile):
        ref, more, at = refs

        def eight(k):
            return jnp.broadcast_to(halo_ref[pl.ds(k * TILES + tile, 1), :], (8, LANES))

        def slots(source, half, row):
            lanes = pl.ds(pl.multiple_of(block * SLOTS + half * LANES, LANES), LANES)
            return source[pl.ds(pl.multiple_of(row, 8), 8), lanes]

        half = eight(at + 1)
        row = (d * 3 + first + g) * 8
        values = jnp.where(half == 0, slots(ref, 0, row), slots(ref, 1, row))
        if wide:
            values = jnp.where(half == 2, slots(more, 0, row), values)
            values = jnp.where(half == 3, slots(more, 1, row), values)
        return gather(values, eight(at))

    def sweep(wide, block, carry):
        low = (left_ref, left_more, 0)
        high = (right_ref, right_more, 2)
        steps = count[block]
        for kmax in range(1, KMAX + 1):

            @pl.when(steps == kmax)
            def _():
                for j in range(4):
                    tile = 4 * block + j
                    drive = speed[pl.ds(tile, 1), :]
                    sine = [
                        sines[pl.ds(k * TILES + tile, 1), :] for k in range(KMAX - kmax, FACES - (KMAX - kmax))
                    ]
                    for g in range(groups):
                        group = first + g
                        base = refr_ref[pl.ds(pl.multiple_of(group * 256 + tile * 8, 8), 8), :] * drive
                        cells = []
                        for c in range(KMAX - kmax, D_LOC + KMAX + kmax):
                            d = c % D_LOC
                            if c < KMAX:
                                cells.append(halo(wide, d, g, block, low, tile))
                            elif c < KMAX + D_LOC:
                                cells.append(x_ref[pl.ds(g * 8 * ROWS + tile * D_LOC + d, 8, stride=ROWS), :])
                            else:
                                cells.append(halo(wide, d, g, block, high, tile))
                        face = [base * v for v in sine]
                        plus = [jnp.maximum(v, 0.0) for v in face]
                        minus = [jnp.minimum(v, 0.0) for v in face]
                        for step in range(kmax):
                            n = len(cells) - 1
                            flux = [
                                plus[step + i] * cells[i] + minus[step + i] * cells[i + 1] for i in range(n)
                            ]
                            cells = [cells[i + 1] - (flux[i + 1] - flux[i]) for i in range(n - 1)]
                        for d in range(D_LOC):
                            y_ref[pl.ds(g * 8 * ROWS + tile * D_LOC + d, 8, stride=ROWS), :] = cells[d]

        return carry

    @pl.when(overflow)
    def _():
        pltpu.sync_copy(left_hbm, left_more)
        pltpu.sync_copy(right_hbm, right_more)
        lax.fori_loop(0, 8, functools.partial(sweep, True), 0)

    @pl.when(jnp.logical_not(overflow))
    def _():
        lax.fori_loop(0, 8, functools.partial(sweep, False), 0)

    if edge:
        for m in range(KMAX):
            row = jnp.where(meta[1] == 0, 7 - m, m)
            rim_ref[m * ROWS : (m + 1) * ROWS, :] = y_ref[pl.ds(pl.multiple_of(row * ROWS, ROWS), ROWS), :]


def shift_kernel(rim, meta, count, note_ref, other_ref, near_ref, far_ref, shift_ref, wave_ref, wet_ref, *rest):
    if rim:
        rim_ref, _, out_hbm, wets, out_ref, sems = rest
    else:
        out_hbm, wets, out_ref, sems = rest
    note = jnp.maximum(note_ref[0:1, :], other_ref[0:1, :])
    peak = jnp.max(jnp.where(iota((1, LANES), 1) == 1, note, LOW))
    wets[...] = wet_ref[...].astype(f32)
    scale = 0.5 / (jnp.full((8, LANES), peak, f32) + EPSILON)
    upper_rows = iota((8, LANES), 0) < D_LOC

    def spread(ref, first, second):
        return jnp.where(upper_rows, ref[pl.ds(first, 1), :], ref[pl.ds(second, 1), :])

    def one(lower, pair, carry):
        tile = 2 * pair
        offset = pl.multiple_of(pair * 8, 8)
        eights = pl.multiple_of(tile * 8, 8)
        drive = wave_ref[pl.ds(offset, 8), :] * scale
        forward = drive > 0.0
        mask_wet = spread(wets, tile, tile + 1)

        def coefficient(g):
            if g >= F_LOC:
                at = 8 + (g - F_LOC) * TILES + tile
                return spread(other_ref, at, at + 1)
            f = g if lower else F_LOC - 1 - g
            at = (f // 8) * 256 + f % 8 + eights
            return spread(shift_ref, at, at + 8)

        def cell(g):
            if g >= F_LOC:
                ref, row = rim_ref, g - F_LOC
            elif g < 16:
                ref, row = far_ref, (g if lower else 15 - g)
            else:
                ref, row = near_ref, (g - 16 if lower else 23 - g)
            return ref[pl.ds(row * ROWS + offset, 8), :]

        steps = count[pair // 2]
        for kmax in range(1, KMAX + 1):

            @pl.when(steps == kmax)
            def _():
                which = range(16 - kmax, F_LOC + kmax) if rim else range(16 + kmax)
                cells = [cell(g) for g in which]
                coefs = [coefficient(g) for g in which]
                face = [(coefs[i] + coefs[i + 1]) * drive for i in range(len(coefs) - 1)]
                for step in range(kmax):
                    n = len(cells)
                    used = face[step:] if rim else face
                    flux = [used[i] * jnp.where(forward, cells[i], cells[i + 1]) for i in range(n - 1)]
                    inner = [cells[i] - (flux[i] - flux[i - 1]) for i in range(1, n - 1)]
                    cells = inner if rim else [cells[0] - flux[0]] + inner
                count_out = 8 if rim else 16
                for i in range(count_out):
                    row = i if lower else count_out - 1 - i
                    out_ref[pl.ds(row * ROWS + offset, 8), :] = cells[i] * mask_wet

        return carry

    @pl.when(meta[1] == 0)
    def _():
        lax.fori_loop(0, TILES // 2, functools.partial(one, True), 0)

    @pl.when(meta[1] == 1)
    def _():
        lax.fori_loop(0, TILES // 2, functools.partial(one, False), 0)

    (copy,) = fetch(((out_ref, rows_of(out_hbm, rim, meta)),), sems)
    copy.wait()


SMEM = pl.BlockSpec(memory_space=pltpu.SMEM)
VMEM = pl.BlockSpec(memory_space=pltpu.VMEM)
ANY = pl.BlockSpec(memory_space=pl.ANY)
HBM = pl.BlockSpec(memory_space=pltpu.HBM)


def call(body, outs, in_specs, scratch, args, out_specs=None, aliases=None):
    return pl.pallas_call(
        body,
        out_shape=outs,
        in_specs=in_specs,
        out_specs=out_specs if out_specs is not None else [VMEM] * len(outs),
        scratch_shapes=scratch,
        input_output_aliases=aliases or {},
        compiler_params=pltpu.CompilerParams(vmem_limit_bytes=VMEM_LIMIT),
        cost_estimate=pl.CostEstimate(flops=0, bytes_accessed=0, transcendentals=0),
    )(*args)


def in_hbm(*arrays):
    return [pltpu.with_memory_space_constraint(a, pltpu.HBM) for a in arrays]


def shape(*dims):
    return jax.ShapeDtypeStruct(dims, f32)


def local(action, bathymetry, refraction, shifting, heading, slope_angle, wet_mask, substeps):
    pts = lax.axis_index(("pts_0", "pts_1"))
    dir_index, freq_index = lax.axis_index("dir"), lax.axis_index("freq")
    meta = jnp.stack([dir_index, freq_index, pts, pts]).astype(i32)
    table = jnp.asarray(angle_table())
    x = action.reshape(F_LOC, D_LOC, TILES, LANES).transpose(0, 2, 1, 3).reshape(F_LOC * ROWS, LANES)
    bath, head, slope, wet = (
        a.reshape(TILES, LANES) for a in (bathymetry, heading, slope_angle, wet_mask)
    )

    def by_eight(a):
        return a.reshape(3, 8, TILES, LANES).transpose(0, 2, 1, 3).reshape(3 * TILES * 8, LANES)

    refr, shift = by_eight(refraction), by_eight(shifting)
    count = lax.axis_size("dir")
    ring_up = [(i, (i + 1) % count) for i in range(count)]
    ring_down = [((i + 1) % count, i) for i in range(count)]
    swap = [(0, 1), (1, 0)]

    wave = [shape(D_LOC * F_LOC, 8 * SLOTS)] * 2
    row = pltpu.VMEM((TILES, LANES), f32)
    row_int = pltpu.VMEM((TILES, LANES), i32)

    def exchange(up, down):
        return lax.ppermute(up, "dir", ring_up), lax.ppermute(down, "dir", ring_down)

    small = [row, row, row_int]
    coefs = pltpu.VMEM((3 * TILES * 8, LANES), f32)
    dma = pltpu.SemaphoreType.DMA
    packed = pltpu.VMEM((D_LOC * F_LOC, 8 * SLOTS), f32)
    up, down = call(
        pack_kernel,
        wave,
        [SMEM, SMEM] + [HBM] * 4,
        small + [pltpu.VMEM((F_LOC, ROWS, LANES), f32), packed, packed, dma((3,)), dma((4,)), dma((4,)), dma((4,))] + [row_int] * 4,
        (meta, table, *in_hbm(bath, slope, wet, x.reshape(F_LOC, ROWS, LANES))),
        out_specs=[ANY, ANY],
    )
    left, right = exchange(up, down)
    note, halo, sines, waves, shift_rim = call(
        note_kernel,
        [
            shape(8, LANES),
            jax.ShapeDtypeStruct((4 * TILES, LANES), i32),
            shape(FACES * TILES, LANES),
            shape(ROWS, LANES),
            shape(KMAX * TILES, LANES),
        ],
        [SMEM] * 3 + [HBM] * 6,
        small
        + [row, coefs, coefs, dma((6,)), row, row]
        + [pltpu.VMEM((8, LANES), f32), pltpu.VMEM((16 * TILES, LANES), f32)],
        (meta, table, substeps, *in_hbm(bath, slope, wet, head, refr, shift)),
    )
    for axis in ("pts_0", "pts_1"):
        note = lax.pmax(note, axis)
    other = lax.ppermute(jnp.concatenate([note, shift_rim], axis=0), "freq", swap)

    def second_wave():
        return exchange(
            *call(
                more_kernel,
                wave,
                [SMEM, SMEM] + [VMEM] * 4,
                [row_int] * 4,
                (meta, table, x, bath, slope, wet),
            )
        )

    def no_wave():
        return tuple(call(lambda *refs: None, wave, [], [], (), out_specs=[ANY, ANY]))

    left_more, right_more = lax.cond(note[0, 2] > SLOTS, second_wave, no_wave)

    def turn(edge):
        groups = 1 if edge else 2
        outs = [shape(groups * 8 * ROWS, LANES)] + ([shape(KMAX * ROWS, LANES)] if edge else [])
        own = [pltpu.VMEM((groups * 8 * ROWS, LANES), f32), dma((1,))]
        return call(
            functools.partial(turn_kernel, edge),
            outs,
            [SMEM] * 2 + [VMEM] * 2 + [HBM] + [VMEM] * 7 + [ANY] * 2,
            [row, packed, packed] + own,
            (meta, substeps, note, other, *in_hbm(x), bath, wet, refr, halo, sines, left, right, left_more, right_more),
        )

    near, rim = turn(True)
    other_rim = lax.ppermute(rim, "freq", swap)
    (far,) = turn(False)

    def shifted_part(rim, more):
        groups = 1 if rim else 2
        (out,) = call(
            functools.partial(shift_kernel, rim),
            [shape(F_LOC * ROWS, LANES)],
            [SMEM] * 2 + [VMEM] * 7 + [VMEM, ANY][: len(more)],
            [row, pltpu.VMEM((groups * 8 * ROWS, LANES), f32), dma((1,))],
            (meta, substeps, note, other, near, far, shift, waves, wet, *more),
            out_specs=[ANY],
            aliases={10: 0} if rim else None,
        )
        return out

    out = shifted_part(True, (other_rim, shifted_part(False, ())))
    return out.reshape(F_LOC, TILES, D_LOC, LANES).transpose(0, 2, 1, 3).reshape(F_LOC, D_LOC, TILES * LANES)


PTS = ("pts_0", "pts_1")


def solution(mesh):
    torus = Mesh(
        mesh.devices.reshape(8, 2, mesh.shape["dir"], mesh.shape["freq"]),
        ("pts_0", "pts_1", "dir", "freq"),
    )
    in_specs = (
        P("freq", "dir", PTS),
        P(PTS),
        P("freq", PTS),
        P("freq", PTS),
        P(PTS),
        P(PTS),
        P(PTS),
        P(PTS),
    )
    return jax.shard_map(local, mesh=torus, in_specs=in_specs, out_specs=P("freq", "dir", PTS), check_vma=False)
```

```python
import functools
import math

import jax
import jax.numpy as jnp
import numpy as np
from jax import lax
from jax.experimental import pallas as pl
from jax.experimental.pallas import tpu as pltpu
from jax.sharding import Mesh
from jax.sharding import PartitionSpec as P

FREQ = 48
DIR = 64
KMAX = 4
BLK = 512
GROUPS = 13
EPSILON = 1e-06
LANES = 128
F_LOC = 24
D_LOC = 4
TILES = 32
SIDE = D_LOC * 24
ROWS = TILES * D_LOC
VMEM_LIMIT = 12 * 1024 * 1024
LOW = -3.0e38

f32, bf16, i32 = jnp.float32, jnp.bfloat16, jnp.int32


def angle_table():
    step = 2.0 * math.pi / DIR
    half = np.arange(DIR // 2) * step
    centre = (np.arange(DIR // 2) + 0.5) * step
    parts = [np.sin(half), np.cos(half), np.sin(centre), np.cos(centre)]
    return np.concatenate([np.concatenate([p, -p]) for p in parts]).astype(np.float32)


SIN_FACE, COS_FACE, SIN_CELL, COS_CELL = 0, DIR, 2 * DIR, 3 * DIR
COS_HALF = math.cos(math.pi / DIR)
FACES = D_LOC + 2 * KMAX - 1


def iota(shape, dim):
    return lax.broadcasted_iota(i32, shape, dim)


def shifted(bath):
    lane = iota((TILES, LANES), 1)
    left = pltpu.roll(bath, 1, 1)
    left = jnp.where(lane == 0, pltpu.roll(left, 1, 0), left)
    right = pltpu.roll(bath, LANES - 1, 1)
    right = jnp.where(lane == LANES - 1, pltpu.roll(right, TILES - 1, 0), right)
    return left, right


def end_points():
    point = iota((TILES, LANES), 0) * LANES + iota((TILES, LANES), 1)
    return point == 0, point == TILES * LANES - 1


def face_sine(table, face, sin_s, cos_s):
    at = lax.rem(face + DIR, DIR)
    return table[SIN_FACE + at] * cos_s - table[COS_FACE + at] * sin_s


def masks(table, bath, wet, sin_s, cos_s):
    left, right = shifted(bath)
    drive = (right - left) * wet
    first, last = end_points()
    ends = first | last

    def at(face):
        speed = drive * face_sine(table, face, sin_s, cos_s)
        return (speed > 0.0) | ends, (speed < 0.0) | ends

    return at


def ranks(first_mask, second_mask):
    first = jnp.where(first_mask, 1.0, 0.0).astype(f32)
    second = jnp.where(second_mask, 1.0, 0.0).astype(f32)
    on = jnp.concatenate([first, second], axis=0).astype(bf16)
    none = jnp.zeros((TILES, LANES), f32)
    spread = jnp.concatenate([first, none, second, none], axis=0).astype(bf16)
    row, col = iota((LANES, LANES), 0), iota((LANES, LANES), 1)
    before = jnp.where(row < col, 1.0, 0.0).astype(bf16)
    earlier = jnp.where((row < col) & (row // 64 == col // 64), 1.0, 0.0).astype(bf16)
    ones = jnp.ones((LANES, LANES), bf16)
    r, c = iota((2 * TILES, 2 * TILES), 0), iota((2 * TILES, 2 * TILES), 1)
    above = jnp.where((c < r) & (r // TILES == c // TILES), 1.0, 0.0).astype(bf16)
    inner = jnp.dot(on, before, preferred_element_type=f32)
    number = jnp.dot(on, ones, preferred_element_type=f32)
    offset = jnp.dot(above, on, preferred_element_type=f32)
    offset = jnp.dot(offset.astype(bf16), ones, preferred_element_type=f32)
    along = lax.dot_general(ones[:16], spread, (((1,), (1,)), ((), ())), preferred_element_type=f32)
    along = jnp.dot(along.astype(bf16), earlier, preferred_element_type=f32)[0:8]
    return inner.astype(i32), offset.astype(i32), number.astype(i32), along.astype(i32)


def gather(x, index):
    return jnp.take_along_axis(x, index, axis=1)


def packing(up_mask, down_mask, source_ref, code_ref, group_ref):
    inner, offset, number, along = ranks(up_mask, down_mask)
    lane = iota((2 * TILES, LANES), 1)
    mark = lane * 129 + 65536
    on = jnp.concatenate([jnp.where(m, 1, 0) for m in (up_mask, down_mask)], axis=0)
    code = jnp.where(on == 1, mark - inner * 128, 0)
    for bit in range(7):
        step = 1 << bit
        far = pltpu.roll(code, LANES - step, 1)
        comes = (far & (128 << bit)) != 0
        goes = (code & (128 << bit)) != 0
        code = jnp.where(comes, far - (128 << bit), jnp.where(goes, 0, code))
    source = gather((code & 127).astype(f32), (lane - offset) & 127)
    source_ref[...] = source.astype(i32)
    start = offset & 127
    here = (lane >= start) & (lane < start + number)
    crosses = (start + number) >= LANES
    code_ref[...] = jnp.where(here, 1, 0) + jnp.where(crosses, 2, 0)
    group_ref[...] = along >> 7


def pack_kernel(wave, meta, table, bath_hbm, slope_hbm, wet_hbm, x_hbm, up_hbm, down_hbm, *rest):
    if wave == 0:
        edge_ref, *rest = rest
    *rest, x_ref = rest
    bath_ref, slope_ref, wet_ref, up_ref, down_ref, sems, in_sems, up_sems, down_sems, at_sems, edge_sem, *rest = rest
    source_ref, code_ref, group_ref, group_at = rest
    begin, size = ((0, GROUPS), (GROUPS, TILES - GROUPS))[wave]

    def arrival(g):
        rows = pl.ds(g * 8 * ROWS, 8 * ROWS)
        return pltpu.make_async_copy(x_hbm.at[rows, :], x_ref.at[rows, :], in_sems.at[g])

    def departures(g):
        rows, columns = pl.ds(g * 8 * D_LOC, 8 * D_LOC), pl.ds(begin * LANES, size * LANES)
        return (
            pltpu.make_async_copy(up_ref.at[rows, columns], up_hbm.at[rows, :], up_sems.at[g]),
            pltpu.make_async_copy(down_ref.at[rows, columns], down_hbm.at[rows, :], down_sems.at[g]),
        )

    copies = fetch(((bath_hbm, bath_ref), (slope_hbm, slope_ref), (wet_hbm, wet_ref)), sems)
    for g in range(3):
        arrival(g).start()
    if wave == 0:
        (kept,) = fetch(((rows_of(x_hbm, True, meta), edge_ref),), edge_sem)
    for ref in (up_ref, down_ref):
        ref[:, begin * LANES : (begin + size) * LANES] = jnp.zeros((SIDE, size * LANES), f32)
    for copy in copies:
        copy.wait()
    slope = slope_ref[...]
    at = masks(table, bath_ref[...], wet_ref[...].astype(f32), jnp.sin(slope), jnp.cos(slope))
    packing(at(D_LOC * meta[0] + D_LOC)[0], at(D_LOC * meta[0])[1], source_ref, code_ref, group_ref)
    (copy,) = fetch(((group_ref, group_at),), at_sems)
    copy.wait()
    sides = (up_ref, down_ref)
    for g in range(3):
        arrival(g).wait()

        def one(tile, partial):
            x = [x_ref[pl.ds(g * 8 * ROWS + tile * D_LOC + d, 8, stride=ROWS), :] for d in range(D_LOC)]
            out = []
            for k, ref in enumerate(sides):
                index = jnp.broadcast_to(source_ref[pl.ds(k * TILES + tile, 1), :], (8, LANES))
                flags = jnp.broadcast_to(code_ref[pl.ds(k * TILES + tile, 1), :], (8, LANES))
                here, crosses = (flags & 1) != 0, flags >= 2
                columns = pl.ds(pl.multiple_of(group_at[0, k * 64 + tile] * LANES, LANES), LANES)
                for d in range(D_LOC):
                    taken = gather(x[d], index)
                    full = jnp.where(here, taken, partial[k * D_LOC + d])
                    ref[(g * D_LOC + d) * 8 : (g * D_LOC + d + 1) * 8, columns] = full
                    out.append(jnp.where(crosses, taken, full))
            return tuple(out)

        def four(i, partial):
            for j in range(4):
                partial = one(4 * i + j, partial)
            return partial

        partial = lax.fori_loop(0, TILES // 4, four, (jnp.zeros((8, LANES), f32),) * (2 * D_LOC))
        for k, ref in enumerate(sides):
            columns = pl.ds(pl.multiple_of(group_at[0, k * 64 + TILES] * LANES, LANES), LANES)
            for d in range(D_LOC):
                ref[(g * D_LOC + d) * 8 : (g * D_LOC + d + 1) * 8, columns] = partial[k * D_LOC + d]
        for copy in departures(g):
            copy.start()
    for g in range(3):
        for copy in departures(g):
            copy.wait()
    if wave == 0:
        kept.wait()


def part(edge, meta):
    return (2 * (1 - meta[1]), 1) if edge else (meta[1], 2)


def rows_of(x_hbm, edge, meta):
    first, groups = part(edge, meta)
    return x_hbm.at[pl.ds(pl.multiple_of(first * 8 * ROWS, 8 * ROWS), groups * 8 * ROWS), :]


def fetch(pairs, sems):
    copies = [pltpu.make_async_copy(source, target, sems.at[i]) for i, (source, target) in enumerate(pairs)]
    for copy in copies:
        copy.start()
    return copies


def note_kernel(meta, table, count, bath_hbm, slope_hbm, wet_hbm, heading_hbm, refr_hbm, shift_hbm, note_ref, halo_ref, group_ref, sine_ref, wave_ref, shift_rim_ref, bath_ref, slope_ref, wet_ref, heading_ref, refr_ref, shift_ref, sems, turn_row, shift_row, refr_row, marks):
    copies = fetch(
        (
            (bath_hbm, bath_ref),
            (slope_hbm, slope_ref),
            (wet_hbm, wet_ref),
            (heading_hbm, heading_ref),
            (refr_hbm, refr_ref),
            (shift_hbm, shift_ref),
        ),
        sems,
    )
    for copy in copies[:4]:
        copy.wait()
    wet, bath = wet_ref[...].astype(f32), bath_ref[...]
    slope, heading = slope_ref[...], heading_ref[...]
    sin_s, cos_s, sin_h, cos_h = jnp.sin(slope), jnp.cos(slope), jnp.sin(heading), jnp.cos(heading)
    at = masks(table, bath, wet, sin_s, cos_s)
    sin_peak = jnp.zeros((TILES, LANES), f32)
    cos_peak = jnp.zeros((TILES, LANES), f32)
    for d in range(DIR // 2):
        sin_a, cos_a = table[SIN_CELL + d], table[COS_CELL + d]
        sin_peak = jnp.maximum(sin_peak, jnp.abs(sin_a * cos_s - cos_a * sin_s))
        cos_peak = jnp.maximum(cos_peak, jnp.abs(cos_a * cos_h + sin_a * sin_h))
    left, right = shifted(bath)
    first, last = end_points()
    gradient = jnp.where(first | last, 0.0, (right - left) * 0.5)
    turn_row[...] = jnp.abs(gradient) * wet * sin_peak
    shift_row[...] = wet * cos_peak
    turn = jnp.zeros((8, LANES), f32)
    shift = jnp.zeros((8, LANES), f32)
    ends = []
    for copy in copies[4:]:
        copy.wait()
    for t in range(TILES):
        coef, shift_coef = turn_row[t : t + 1, :], shift_row[t : t + 1, :]
        most, most_shift = jnp.zeros((8, LANES), f32), jnp.zeros((8, LANES), f32)
        for k in range(3):
            rows = slice(k * 256 + t * 8, k * 256 + t * 8 + 8)
            most = jnp.maximum(most, jnp.abs(refr_ref[rows, :]))
            most_shift = jnp.maximum(most_shift, jnp.abs(shift_ref[rows, :]))
        turn = jnp.maximum(turn, most * coef)
        shift = jnp.maximum(shift, most_shift * shift_coef)
        if t in (0, TILES - 1):
            ends.append(jnp.max(most, axis=0, keepdims=True))
    for i in range(8):
        low, high = at(D_LOC * i)
        marks[2 * i * TILES : (2 * i + 1) * TILES, :] = jnp.where(low, 1.0, 0.0).astype(f32)
        marks[(2 * i + 1) * TILES : (2 * i + 2) * TILES, :] = jnp.where(high, 1.0, 0.0).astype(f32)
    ones = jnp.ones((LANES, LANES), bf16)
    group = jnp.where(iota((16, 16 * TILES), 0) == iota((16, 16 * TILES), 1) // TILES, 1.0, 0.0).astype(bf16)
    per_side = jnp.dot(group, marks[...].astype(bf16), preferred_element_type=f32)
    per_side = jnp.dot(per_side.astype(bf16), ones, preferred_element_type=f32)

    weight = wet * sin_peak
    row, lane = iota((8, LANES), 0), iota((8, LANES), 1)
    note = jnp.where(row == 0, jnp.where(lane == 0, jnp.max(turn), jnp.max(shift)), LOW)
    note = jnp.where((row == 0) & (lane == 2), jnp.max(per_side), note)
    refr_row[0:1, :] = ends[0] * weight[0:1, :]
    refr_row[1:2, :] = ends[1] * weight[TILES - 1 : TILES, :]
    mine = lane == meta[2]
    for r, value in enumerate(
        (
            bath_ref[0:1, 0:1],
            bath_ref[0:1, 1:2],
            bath_ref[TILES - 1 : TILES, LANES - 2 : LANES - 1],
            bath_ref[TILES - 1 : TILES, LANES - 1 : LANES],
            refr_row[0:1, 0:1],
            refr_row[1:2, LANES - 1 : LANES],
        )
    ):
        note = jnp.where((row == 1 + r) & mine, value, note)
    note_ref[...] = note
    first = 2 * (1 - meta[1])
    for m in range(KMAX):
        row = jnp.where(meta[1] == 0, 7 - m, m)
        shift_rim_ref[m * TILES : (m + 1) * TILES, :] = shift_ref[pl.ds(first * 256 + row, TILES, stride=8), :]

    inner, offset, _, along = ranks(at(D_LOC * meta[0])[0], at(D_LOC * meta[0] + D_LOC)[1])
    halo_ref[: 2 * TILES, :] = (inner + offset) & 127
    halo_ref[2 * TILES :, :] = jnp.where(iota((2 * TILES, LANES), 1) >= (offset & 127), 1, 0)
    group_ref[...] = along >> 7
    for k in range(FACES):
        sine_ref[k * TILES : (k + 1) * TILES, :] = face_sine(table, D_LOC * meta[0] - KMAX + 1 + k, sin_s, cos_s)
    sign = jnp.where(meta[1] == 0, 0.5, -0.5)
    speed = wet * sign / block_counts(count)
    for d in range(D_LOC):
        sin_a, cos_a = table[SIN_CELL + D_LOC * meta[0] + d], table[COS_CELL + D_LOC * meta[0] + d]
        wave_ref[pl.ds(d, TILES, stride=D_LOC), :] = (cos_a * cos_h + sin_a * sin_h) * speed


def full_gradient(meta, note, bath):
    row, lane = iota((8, LANES), 0), iota((8, LANES), 1)
    below = jnp.max(jnp.where((row == 4) & (lane == meta[2] - 1), note, LOW))
    above = jnp.max(jnp.where((row == 1) & (lane == meta[2] + 1), note, LOW))
    left, right = shifted(bath)
    first, last = end_points()
    left = jnp.where(first, jnp.where(meta[2] == 0, bath, below), left)
    right = jnp.where(last, jnp.where(meta[2] == 15, bath, above), right)
    return (right - left) * 0.5


def largest_turn(note):
    lane = iota((1, LANES), 1)
    first, second, second_last, last = (note[r : r + 1, :] for r in range(1, 5))
    below = jnp.where(lane == 0, first, pltpu.roll(jnp.broadcast_to(last, (8, LANES)), 1, 1)[0:1, :])
    above = jnp.where(lane == 15, last, pltpu.roll(jnp.broadcast_to(first, (8, LANES)), LANES - 1, 1)[0:1, :])
    at_first = jnp.abs(second - below) * 0.5 * note[5:6, :]
    at_last = jnp.abs(above - second_last) * 0.5 * note[6:7, :]
    here = jnp.where(lane < 16, jnp.maximum(at_first, at_last), 0.0)
    return jnp.maximum(jnp.max(here), jnp.max(jnp.where(lane == 0, note[0:1, :], 0.0)))


def block_counts(count):
    tile_block = iota((TILES, LANES), 0) // 4
    counts = jnp.zeros((TILES, LANES), i32)
    for b in range(8):
        counts = jnp.where(tile_block == b, count[b], counts)
    return counts.astype(f32)


def turn_kernel(edge, meta, count, group_at, note_ref, other_ref, x_hbm, bath_ref, wet_ref, refr_ref, halo_ref, sines, left_ref, right_ref, left_hbm, right_hbm, *rest):
    if edge:
        y_ref, rim_ref, *rest = rest
    else:
        y_ref, *rest = rest
    if edge:
        x_ref = x_hbm
    else:
        *rest, x_ref, sems = rest
        (copy,) = fetch(((rows_of(x_hbm, edge, meta), x_ref),), sems)
    speed, left_wide, right_wide = rest
    note = jnp.maximum(note_ref[...], other_ref[0:8, :])
    scale = 0.5 / (jnp.full((TILES, LANES), largest_turn(note), f32) + EPSILON)
    wet = wet_ref[...].astype(f32)
    speed[...] = full_gradient(meta, note, bath_ref[...]) * wet * scale * COS_HALF / block_counts(count)
    first, groups = part(edge, meta)
    if not edge:
        copy.wait()
    overflow = jnp.max(jnp.where(iota((1, LANES), 1) == 2, note[0:1, :], LOW)) > GROUPS * LANES

    def halo(wide, d, g, refs, tile):
        ref, side = refs
        most = TILES - 1 if wide else GROUPS - 1

        def eight(k):
            return jnp.broadcast_to(halo_ref[pl.ds(k * TILES + tile, 1), :], (8, LANES))

        def slots(group):
            lanes = pl.ds(pl.multiple_of(jnp.minimum(group, most) * LANES, LANES), LANES)
            return ref[pl.ds(pl.multiple_of(((first + g) * D_LOC + d) * 8, 8), 8), lanes]

        group = group_at[0, side * 64 + tile]
        values = jnp.where(eight(2 + side) == 1, slots(group), slots(group + 1))
        return gather(values, eight(side))

    def sweep(wide, block, carry):
        low = (left_wide if wide else left_ref, 0)
        high = (right_wide if wide else right_ref, 1)
        steps = count[block]
        for kmax in range(1, KMAX + 1):

            @pl.when(steps == kmax)
            def _():
                for j in range(4):
                    tile = 4 * block + j
                    drive = speed[pl.ds(tile, 1), :]
                    sine = [
                        sines[pl.ds(k * TILES + tile, 1), :] for k in range(KMAX - kmax, FACES - (KMAX - kmax))
                    ]
                    for g in range(groups):
                        group = first + g
                        base = refr_ref[pl.ds(pl.multiple_of(group * 256 + tile * 8, 8), 8), :] * drive
                        cells = []
                        for c in range(KMAX - kmax, D_LOC + KMAX + kmax):
                            d = c % D_LOC
                            if c < KMAX:
                                cells.append(halo(wide, d, g, low, tile))
                            elif c < KMAX + D_LOC:
                                cells.append(x_ref[pl.ds(g * 8 * ROWS + tile * D_LOC + d, 8, stride=ROWS), :])
                            else:
                                cells.append(halo(wide, d, g, high, tile))
                        face = [base * v for v in sine]
                        plus = [jnp.maximum(v, 0.0) for v in face]
                        minus = [jnp.minimum(v, 0.0) for v in face]
                        for step in range(kmax):
                            n = len(cells) - 1
                            flux = [
                                plus[step + i] * cells[i] + minus[step + i] * cells[i + 1] for i in range(n)
                            ]
                            cells = [cells[i + 1] - (flux[i + 1] - flux[i]) for i in range(n - 1)]
                        for d in range(D_LOC):
                            y_ref[pl.ds(g * 8 * ROWS + tile * D_LOC + d, 8, stride=ROWS), :] = cells[d]

        return carry

    @pl.when(overflow)
    def _():
        for ref, more, whole in ((left_ref, left_hbm, left_wide), (right_ref, right_hbm, right_wide)):
            whole[:, : GROUPS * LANES] = ref[...]
            pltpu.sync_copy(more, whole.at[:, GROUPS * LANES :])
        lax.fori_loop(0, 8, functools.partial(sweep, True), 0)

    @pl.when(jnp.logical_not(overflow))
    def _():
        lax.fori_loop(0, 8, functools.partial(sweep, False), 0)

    if edge:
        for m in range(KMAX):
            row = jnp.where(meta[1] == 0, 7 - m, m)
            rim_ref[m * ROWS : (m + 1) * ROWS, :] = y_ref[pl.ds(pl.multiple_of(row * ROWS, ROWS), ROWS), :]


def shift_kernel(rim, meta, count, note_ref, other_ref, near_ref, far_ref, shift_ref, wave_ref, wet_ref, *rest):
    if rim:
        rim_ref, _, out_hbm, wets, out_ref, sems = rest
    else:
        out_hbm, wets, out_ref, sems = rest
    note = jnp.maximum(note_ref[0:1, :], other_ref[0:1, :])
    peak = jnp.max(jnp.where(iota((1, LANES), 1) == 1, note, LOW))
    wets[...] = wet_ref[...].astype(f32)
    scale = 0.5 / (jnp.full((8, LANES), peak, f32) + EPSILON)
    upper_rows = iota((8, LANES), 0) < D_LOC

    def spread(ref, first, second):
        return jnp.where(upper_rows, ref[pl.ds(first, 1), :], ref[pl.ds(second, 1), :])

    def one(lower, pair, carry):
        tile = 2 * pair
        offset = pl.multiple_of(pair * 8, 8)
        eights = pl.multiple_of(tile * 8, 8)
        drive = wave_ref[pl.ds(offset, 8), :] * scale
        forward = drive > 0.0
        mask_wet = spread(wets, tile, tile + 1)

        def coefficient(g):
            if g >= F_LOC:
                at = 8 + (g - F_LOC) * TILES + tile
                return spread(other_ref, at, at + 1)
            f = g if lower else F_LOC - 1 - g
            at = (f // 8) * 256 + f % 8 + eights
            return spread(shift_ref, at, at + 8)

        def cell(g):
            if g >= F_LOC:
                ref, row = rim_ref, g - F_LOC
            elif g < 16:
                ref, row = far_ref, (g if lower else 15 - g)
            else:
                ref, row = near_ref, (g - 16 if lower else 23 - g)
            return ref[pl.ds(row * ROWS + offset, 8), :]

        steps = count[pair // 2]
        for kmax in range(1, KMAX + 1):

            @pl.when(steps == kmax)
            def _():
                which = range(16 - kmax, F_LOC + kmax) if rim else range(16 + kmax)
                cells = [cell(g) for g in which]
                coefs = [coefficient(g) for g in which]
                face = [(coefs[i] + coefs[i + 1]) * drive for i in range(len(coefs) - 1)]
                for step in range(kmax):
                    n = len(cells)
                    used = face[step:] if rim else face
                    flux = [used[i] * jnp.where(forward, cells[i], cells[i + 1]) for i in range(n - 1)]
                    inner = [cells[i] - (flux[i] - flux[i - 1]) for i in range(1, n - 1)]
                    cells = inner if rim else [cells[0] - flux[0]] + inner
                count_out = 8 if rim else 16
                for i in range(count_out):
                    row = i if lower else count_out - 1 - i
                    out_ref[pl.ds(row * ROWS + offset, 8), :] = cells[i] * mask_wet

        return carry

    @pl.when(meta[1] == 0)
    def _():
        lax.fori_loop(0, TILES // 2, functools.partial(one, True), 0)

    @pl.when(meta[1] == 1)
    def _():
        lax.fori_loop(0, TILES // 2, functools.partial(one, False), 0)

    (copy,) = fetch(((out_ref, rows_of(out_hbm, rim, meta)),), sems)
    copy.wait()


SMEM = pl.BlockSpec(memory_space=pltpu.SMEM)
VMEM = pl.BlockSpec(memory_space=pltpu.VMEM)
ANY = pl.BlockSpec(memory_space=pl.ANY)
HBM = pl.BlockSpec(memory_space=pltpu.HBM)


def call(body, outs, in_specs, scratch, args, out_specs=None, aliases=None):
    return pl.pallas_call(
        body,
        out_shape=outs,
        in_specs=in_specs,
        out_specs=out_specs if out_specs is not None else [VMEM] * len(outs),
        scratch_shapes=scratch,
        input_output_aliases=aliases or {},
        compiler_params=pltpu.CompilerParams(vmem_limit_bytes=VMEM_LIMIT),
        cost_estimate=pl.CostEstimate(flops=0, bytes_accessed=0, transcendentals=0),
    )(*args)


def in_hbm(*arrays):
    return [pltpu.with_memory_space_constraint(a, pltpu.HBM) for a in arrays]


def shape(*dims):
    return jax.ShapeDtypeStruct(dims, f32)


def local(action, bathymetry, refraction, shifting, heading, slope_angle, wet_mask, substeps):
    pts = lax.axis_index(("pts_0", "pts_1"))
    dir_index, freq_index = lax.axis_index("dir"), lax.axis_index("freq")
    meta = jnp.stack([dir_index, freq_index, pts, pts]).astype(i32)
    table = jnp.asarray(angle_table())
    x = action.reshape(F_LOC, D_LOC, TILES, LANES).transpose(0, 2, 1, 3).reshape(F_LOC * ROWS, LANES)
    bath, head, slope, wet = (
        a.reshape(TILES, LANES) for a in (bathymetry, heading, slope_angle, wet_mask)
    )

    def by_eight(a):
        return a.reshape(3, 8, TILES, LANES).transpose(0, 2, 1, 3).reshape(3 * TILES * 8, LANES)

    refr, shift = by_eight(refraction), by_eight(shifting)
    count = lax.axis_size("dir")
    ring_up = [(i, (i + 1) % count) for i in range(count)]
    ring_down = [((i + 1) % count, i) for i in range(count)]
    swap = [(0, 1), (1, 0)]

    waves_of = [[shape(SIDE, GROUPS * LANES)] * 2, [shape(SIDE, (TILES - GROUPS) * LANES)] * 2]
    row = pltpu.VMEM((TILES, LANES), f32)
    row_int = pltpu.VMEM((TILES, LANES), i32)

    def exchange(up, down):
        return lax.ppermute(up, "dir", ring_up), lax.ppermute(down, "dir", ring_down)

    small = [row, row, row_int]
    coefs = pltpu.VMEM((3 * TILES * 8, LANES), f32)
    dma = pltpu.SemaphoreType.DMA
    packed = pltpu.VMEM((SIDE, (TILES + 1) * LANES), f32)
    wide = pltpu.VMEM((SIDE, TILES * LANES), f32)

    def pack(wave):
        vmem_x = pltpu.VMEM((F_LOC * ROWS, LANES), f32)
        both = pltpu.VMEM((2 * TILES, LANES), i32)
        return call(
            functools.partial(pack_kernel, wave),
            waves_of[wave] + ([pltpu.VMEM((8 * ROWS, LANES), f32)] if wave == 0 else []),
            [SMEM, SMEM] + [HBM] * 4,
            small
            + [packed, packed, dma((3,)), dma((3,)), dma((3,)), dma((3,)), dma((1,)), dma((1,))]
            + [both, both, pltpu.VMEM((8, LANES), i32), pltpu.SMEM((8, LANES), i32)]
            + [vmem_x],
            (meta, table, *in_hbm(bath, slope, wet, x)),
            out_specs=[ANY, ANY] + ([VMEM] if wave == 0 else []),
        )

    up, down, x_edge = pack(0)
    left, right = exchange(up, down)
    note, halo, groups_at, sines, waves, shift_rim = call(
        note_kernel,
        [
            shape(8, LANES),
            jax.ShapeDtypeStruct((4 * TILES, LANES), i32),
            jax.ShapeDtypeStruct((8, LANES), i32),
            shape(FACES * TILES, LANES),
            shape(ROWS, LANES),
            shape(KMAX * TILES, LANES),
        ],
        [SMEM] * 3 + [HBM] * 6,
        small
        + [row, coefs, coefs, dma((6,)), row, row]
        + [pltpu.VMEM((8, LANES), f32), pltpu.VMEM((16 * TILES, LANES), f32)],
        (meta, table, substeps, *in_hbm(bath, slope, wet, head, refr, shift)),
    )
    for axis in ("pts_0", "pts_1"):
        note = lax.pmax(note, axis)
    other = lax.ppermute(jnp.concatenate([note, shift_rim], axis=0), "freq", swap)

    def second_wave():
        return exchange(*pack(1))

    def no_wave():
        return tuple(call(lambda *refs: None, waves_of[1], [], [], (), out_specs=[ANY, ANY]))

    left_more, right_more = lax.cond(note[0, 2] > GROUPS * LANES, second_wave, no_wave)

    def turn(edge):
        groups = 1 if edge else 2
        outs = [shape(groups * 8 * ROWS, LANES)] + ([shape(KMAX * ROWS, LANES)] if edge else [])
        return call(
            functools.partial(turn_kernel, edge),
            outs,
            [SMEM] * 3 + [VMEM] * 2 + [VMEM if edge else HBM] + [VMEM] * 7 + [HBM] * 2,
            [row, wide, wide] + ([] if edge else [pltpu.VMEM((groups * 8 * ROWS, LANES), f32), dma((1,))]),
            (meta, substeps, groups_at, note, other, *([x_edge] if edge else in_hbm(x)), bath, wet, refr, halo, sines, left, right, *in_hbm(left_more, right_more)),
        )

    near, rim = turn(True)
    other_rim = lax.ppermute(rim, "freq", swap)
    (far,) = turn(False)

    def shifted_part(rim, more):
        groups = 1 if rim else 2
        (out,) = call(
            functools.partial(shift_kernel, rim),
            [shape(F_LOC * ROWS, LANES)],
            [SMEM] * 2 + [VMEM] * 7 + [VMEM, ANY][: len(more)],
            [row, pltpu.VMEM((groups * 8 * ROWS, LANES), f32), dma((1,))],
            (meta, substeps, note, other, near, far, shift, waves, wet, *more),
            out_specs=[ANY],
            aliases={10: 0} if rim else None,
        )
        return out

    out = shifted_part(True, (other_rim, shifted_part(False, ())))
    return out.reshape(F_LOC, TILES, D_LOC, LANES).transpose(0, 2, 1, 3).reshape(F_LOC, D_LOC, TILES * LANES)


PTS = ("pts_0", "pts_1")


def solution(mesh):
    torus = Mesh(
        mesh.devices.reshape(8, 2, mesh.shape["dir"], mesh.shape["freq"]),
        ("pts_0", "pts_1", "dir", "freq"),
    )
    in_specs = (
        P("freq", "dir", PTS),
        P(PTS),
        P("freq", PTS),
        P("freq", PTS),
        P(PTS),
        P(PTS),
        P(PTS),
        P(PTS),
    )
    return jax.shard_map(local, mesh=torus, in_specs=in_specs, out_specs=P("freq", "dir", PTS), check_vma=False)
```

```python
import functools
import math

import jax
import jax.numpy as jnp
import numpy as np
from jax import lax
from jax.experimental import pallas as pl
from jax.experimental.pallas import tpu as pltpu
from jax.sharding import Mesh
from jax.sharding import PartitionSpec as P

FREQ = 48
DIR = 64
KMAX = 4
BLK = 512
GROUPS = 13
EPSILON = 1e-06
LANES = 128
F_LOC = 24
D_LOC = 4
TILES = 32
SIDE = D_LOC * 24
ROWS = TILES * D_LOC
VMEM_LIMIT = 12 * 1024 * 1024
LOW = -3.0e38

f32, bf16, i32 = jnp.float32, jnp.bfloat16, jnp.int32


def angle_table():
    step = 2.0 * math.pi / DIR
    half = np.arange(DIR // 2) * step
    centre = (np.arange(DIR // 2) + 0.5) * step
    parts = [np.sin(half), np.cos(half), np.sin(centre), np.cos(centre)]
    return np.concatenate([np.concatenate([p, -p]) for p in parts]).astype(np.float32)


SIN_FACE, COS_FACE, SIN_CELL, COS_CELL = 0, DIR, 2 * DIR, 3 * DIR
COS_HALF = math.cos(math.pi / DIR)
FACES = D_LOC + 2 * KMAX - 1


def iota(shape, dim):
    return lax.broadcasted_iota(i32, shape, dim)


def shifted(bath):
    lane = iota((TILES, LANES), 1)
    left = pltpu.roll(bath, 1, 1)
    left = jnp.where(lane == 0, pltpu.roll(left, 1, 0), left)
    right = pltpu.roll(bath, LANES - 1, 1)
    right = jnp.where(lane == LANES - 1, pltpu.roll(right, TILES - 1, 0), right)
    return left, right


def end_points():
    point = iota((TILES, LANES), 0) * LANES + iota((TILES, LANES), 1)
    return point == 0, point == TILES * LANES - 1


def face_sine(table, face, sin_s, cos_s):
    at = lax.rem(face + DIR, DIR)
    return table[SIN_FACE + at] * cos_s - table[COS_FACE + at] * sin_s


def masks(table, bath, wet, sin_s, cos_s):
    left, right = shifted(bath)
    drive = (right - left) * wet
    first, last = end_points()
    ends = first | last

    def at(face):
        speed = drive * face_sine(table, face, sin_s, cos_s)
        return (speed > 0.0) | ends, (speed < 0.0) | ends

    return at


def ranks(first_mask, second_mask):
    first = jnp.where(first_mask, 1.0, 0.0).astype(f32)
    second = jnp.where(second_mask, 1.0, 0.0).astype(f32)
    on = jnp.concatenate([first, second], axis=0).astype(bf16)
    none = jnp.zeros((TILES, LANES), f32)
    spread = jnp.concatenate([first, none, second, none], axis=0).astype(bf16)
    row, col = iota((LANES, LANES), 0), iota((LANES, LANES), 1)
    before = jnp.where(row < col, 1.0, 0.0).astype(bf16)
    earlier = jnp.where((row < col) & (row // 64 == col // 64), 1.0, 0.0).astype(bf16)
    ones = jnp.ones((LANES, LANES), bf16)
    r, c = iota((2 * TILES, 2 * TILES), 0), iota((2 * TILES, 2 * TILES), 1)
    above = jnp.where((c < r) & (r // TILES == c // TILES), 1.0, 0.0).astype(bf16)
    inner = jnp.dot(on, before, preferred_element_type=f32)
    number = jnp.dot(on, ones, preferred_element_type=f32)
    offset = jnp.dot(above, on, preferred_element_type=f32)
    offset = jnp.dot(offset.astype(bf16), ones, preferred_element_type=f32)
    along = lax.dot_general(ones[:16], spread, (((1,), (1,)), ((), ())), preferred_element_type=f32)
    along = jnp.dot(along.astype(bf16), earlier, preferred_element_type=f32)[0:8]
    return inner.astype(i32), offset.astype(i32), number.astype(i32), along.astype(i32)


def gather(x, index):
    return jnp.take_along_axis(x, index, axis=1)


def packing(up_mask, down_mask, source_ref, code_ref, group_ref, send_groups):
    inner, offset, number, along = ranks(up_mask, down_mask)
    group_ref[...] = along >> 7
    send_groups()
    lane = iota((2 * TILES, LANES), 1)
    mark = lane * 129 + 65536
    on = jnp.concatenate([jnp.where(m, 1, 0) for m in (up_mask, down_mask)], axis=0)
    code = jnp.where(on == 1, mark - inner * 128, 0)
    for bit in range(7):
        step = 1 << bit
        far = pltpu.roll(code, LANES - step, 1)
        comes = (far & (128 << bit)) != 0
        goes = (code & (128 << bit)) != 0
        code = jnp.where(comes, far - (128 << bit), jnp.where(goes, 0, code))
    source = gather((code & 127).astype(f32), (lane - offset) & 127)
    source_ref[...] = source.astype(i32)
    start = offset & 127
    here = (lane >= start) & (lane < start + number)
    crosses = (start + number) >= LANES
    code_ref[...] = jnp.where(here, 1, 0) + jnp.where(crosses, 2, 0)


def pack_kernel(wave, meta, table, bath_hbm, slope_hbm, wet_hbm, x_hbm, up_hbm, down_hbm, *rest):
    if wave == 0:
        edge_ref, *rest = rest
    *rest, x_ref = rest
    bath_ref, slope_ref, wet_ref, up_ref, down_ref, sems, in_sems, up_sems, down_sems, at_sems, edge_sem, *rest = rest
    source_ref, code_ref, group_ref, group_at = rest
    begin, size = ((0, GROUPS), (GROUPS, TILES - GROUPS))[wave]

    def arrival(g):
        rows = pl.ds(g * 8 * ROWS, 8 * ROWS)
        return pltpu.make_async_copy(x_hbm.at[rows, :], x_ref.at[rows, :], in_sems.at[g])

    def departures(g):
        rows, columns = pl.ds(g * 8 * D_LOC, 8 * D_LOC), pl.ds(begin * LANES, size * LANES)
        return (
            pltpu.make_async_copy(up_ref.at[rows, columns], up_hbm.at[rows, :], up_sems.at[g]),
            pltpu.make_async_copy(down_ref.at[rows, columns], down_hbm.at[rows, :], down_sems.at[g]),
        )

    copies = fetch(((bath_hbm, bath_ref), (slope_hbm, slope_ref), (wet_hbm, wet_ref)), sems)
    for g in range(3):
        arrival(g).start()
    if wave == 0:
        (kept,) = fetch(((rows_of(x_hbm, True, meta), edge_ref),), edge_sem)
    for ref in (up_ref, down_ref):
        ref[:, begin * LANES : (begin + size) * LANES] = jnp.zeros((SIDE, size * LANES), f32)
    for copy in copies:
        copy.wait()
    slope = slope_ref[...]
    at = masks(table, bath_ref[...], wet_ref[...].astype(f32), jnp.sin(slope), jnp.cos(slope))
    copy = pltpu.make_async_copy(group_ref, group_at, at_sems.at[0])
    packing(at(D_LOC * meta[0] + D_LOC)[0], at(D_LOC * meta[0])[1], source_ref, code_ref, group_ref, copy.start)
    copy.wait()
    sides = (up_ref, down_ref)
    for g in range(3):
        arrival(g).wait()

        def four(i, partial):
            tiles = [4 * i + j for j in range(4)]
            taken, flags = [], []
            for tile in tiles:
                x = [x_ref[pl.ds(g * 8 * ROWS + tile * D_LOC + d, 8, stride=ROWS), :] for d in range(D_LOC)]
                for k in range(2):
                    index = jnp.broadcast_to(source_ref[pl.ds(k * TILES + tile, 1), :], (8, LANES))
                    flags.append(jnp.broadcast_to(code_ref[pl.ds(k * TILES + tile, 1), :], (8, LANES)))
                    taken.append([gather(x[d], index) for d in range(D_LOC)])
            for j, tile in enumerate(tiles):
                out = []
                for k, ref in enumerate(sides):
                    here, crosses = (flags[2 * j + k] & 1) != 0, flags[2 * j + k] >= 2
                    columns = pl.ds(pl.multiple_of(group_at[0, k * 64 + tile] * LANES, LANES), LANES)
                    for d in range(D_LOC):
                        value = taken[2 * j + k][d]
                        full = jnp.where(here, value, partial[k * D_LOC + d])
                        ref[(g * D_LOC + d) * 8 : (g * D_LOC + d + 1) * 8, columns] = full
                        out.append(jnp.where(crosses, value, full))
                partial = tuple(out)
            return partial

        partial = lax.fori_loop(0, TILES // 4, four, (jnp.zeros((8, LANES), f32),) * (2 * D_LOC))
        for k, ref in enumerate(sides):
            columns = pl.ds(pl.multiple_of(group_at[0, k * 64 + TILES] * LANES, LANES), LANES)
            for d in range(D_LOC):
                ref[(g * D_LOC + d) * 8 : (g * D_LOC + d + 1) * 8, columns] = partial[k * D_LOC + d]
        for copy in departures(g):
            copy.start()
    for g in range(3):
        for copy in departures(g):
            copy.wait()
    if wave == 0:
        kept.wait()


def part(edge, meta):
    return (2 * (1 - meta[1]), 1) if edge else (meta[1], 2)


def rows_of(x_hbm, edge, meta):
    first, groups = part(edge, meta)
    return x_hbm.at[pl.ds(pl.multiple_of(first * 8 * ROWS, 8 * ROWS), groups * 8 * ROWS), :]


def fetch(pairs, sems):
    copies = [pltpu.make_async_copy(source, target, sems.at[i]) for i, (source, target) in enumerate(pairs)]
    for copy in copies:
        copy.start()
    return copies


def note_kernel(meta, table, count, bath_hbm, slope_hbm, wet_hbm, heading_hbm, refr_hbm, shift_hbm, note_ref, halo_ref, group_ref, sine_ref, wave_ref, shift_rim_ref, bath_ref, slope_ref, wet_ref, heading_ref, refr_ref, shift_ref, sems, turn_row, shift_row, refr_row, marks):
    copies = fetch(
        (
            (bath_hbm, bath_ref),
            (slope_hbm, slope_ref),
            (wet_hbm, wet_ref),
            (heading_hbm, heading_ref),
            (refr_hbm, refr_ref),
            (shift_hbm, shift_ref),
        ),
        sems,
    )
    for copy in copies[:4]:
        copy.wait()
    wet, bath = wet_ref[...].astype(f32), bath_ref[...]
    slope, heading = slope_ref[...], heading_ref[...]
    sin_s, cos_s, sin_h, cos_h = jnp.sin(slope), jnp.cos(slope), jnp.sin(heading), jnp.cos(heading)
    at = masks(table, bath, wet, sin_s, cos_s)
    sin_peak = jnp.zeros((TILES, LANES), f32)
    cos_peak = jnp.zeros((TILES, LANES), f32)
    for d in range(DIR // 2):
        sin_a, cos_a = table[SIN_CELL + d], table[COS_CELL + d]
        sin_peak = jnp.maximum(sin_peak, jnp.abs(sin_a * cos_s - cos_a * sin_s))
        cos_peak = jnp.maximum(cos_peak, jnp.abs(cos_a * cos_h + sin_a * sin_h))
    left, right = shifted(bath)
    first, last = end_points()
    gradient = jnp.where(first | last, 0.0, (right - left) * 0.5)
    turn_row[...] = jnp.abs(gradient) * wet * sin_peak
    shift_row[...] = wet * cos_peak
    turn = jnp.zeros((8, LANES), f32)
    shift = jnp.zeros((8, LANES), f32)
    ends = []
    for copy in copies[4:]:
        copy.wait()
    for t in range(TILES):
        coef, shift_coef = turn_row[t : t + 1, :], shift_row[t : t + 1, :]
        most, most_shift = jnp.zeros((8, LANES), f32), jnp.zeros((8, LANES), f32)
        for k in range(3):
            rows = slice(k * 256 + t * 8, k * 256 + t * 8 + 8)
            most = jnp.maximum(most, jnp.abs(refr_ref[rows, :]))
            most_shift = jnp.maximum(most_shift, jnp.abs(shift_ref[rows, :]))
        turn = jnp.maximum(turn, most * coef)
        shift = jnp.maximum(shift, most_shift * shift_coef)
        if t in (0, TILES - 1):
            ends.append(jnp.max(most, axis=0, keepdims=True))
    for i in range(8):
        low, high = at(D_LOC * i)
        marks[2 * i * TILES : (2 * i + 1) * TILES, :] = jnp.where(low, 1.0, 0.0).astype(f32)
        marks[(2 * i + 1) * TILES : (2 * i + 2) * TILES, :] = jnp.where(high, 1.0, 0.0).astype(f32)
    ones = jnp.ones((LANES, LANES), bf16)
    group = jnp.where(iota((16, 16 * TILES), 0) == iota((16, 16 * TILES), 1) // TILES, 1.0, 0.0).astype(bf16)
    per_side = jnp.dot(group, marks[...].astype(bf16), preferred_element_type=f32)
    per_side = jnp.dot(per_side.astype(bf16), ones, preferred_element_type=f32)

    weight = wet * sin_peak
    row, lane = iota((8, LANES), 0), iota((8, LANES), 1)
    note = jnp.where(row == 0, jnp.where(lane == 0, jnp.max(turn), jnp.max(shift)), LOW)
    note = jnp.where((row == 0) & (lane == 2), jnp.max(per_side), note)
    refr_row[0:1, :] = ends[0] * weight[0:1, :]
    refr_row[1:2, :] = ends[1] * weight[TILES - 1 : TILES, :]
    mine = lane == meta[2]
    for r, value in enumerate(
        (
            bath_ref[0:1, 0:1],
            bath_ref[0:1, 1:2],
            bath_ref[TILES - 1 : TILES, LANES - 2 : LANES - 1],
            bath_ref[TILES - 1 : TILES, LANES - 1 : LANES],
            refr_row[0:1, 0:1],
            refr_row[1:2, LANES - 1 : LANES],
        )
    ):
        note = jnp.where((row == 1 + r) & mine, value, note)
    note_ref[...] = note
    first = 2 * (1 - meta[1])
    for m in range(KMAX):
        row = jnp.where(meta[1] == 0, 7 - m, m)
        shift_rim_ref[m * TILES : (m + 1) * TILES, :] = shift_ref[pl.ds(first * 256 + row, TILES, stride=8), :]

    inner, offset, _, along = ranks(at(D_LOC * meta[0])[0], at(D_LOC * meta[0] + D_LOC)[1])
    halo_ref[: 2 * TILES, :] = (inner + offset) & 127
    halo_ref[2 * TILES :, :] = jnp.where(iota((2 * TILES, LANES), 1) >= (offset & 127), 1, 0)
    group_ref[...] = along >> 7
    for k in range(FACES):
        sine_ref[k * TILES : (k + 1) * TILES, :] = face_sine(table, D_LOC * meta[0] - KMAX + 1 + k, sin_s, cos_s)
    sign = jnp.where(meta[1] == 0, 0.5, -0.5)
    speed = wet * sign / block_counts(count)
    for d in range(D_LOC):
        sin_a, cos_a = table[SIN_CELL + D_LOC * meta[0] + d], table[COS_CELL + D_LOC * meta[0] + d]
        wave_ref[pl.ds(d, TILES, stride=D_LOC), :] = (cos_a * cos_h + sin_a * sin_h) * speed


def full_gradient(meta, note, bath):
    row, lane = iota((8, LANES), 0), iota((8, LANES), 1)
    below = jnp.max(jnp.where((row == 4) & (lane == meta[2] - 1), note, LOW))
    above = jnp.max(jnp.where((row == 1) & (lane == meta[2] + 1), note, LOW))
    left, right = shifted(bath)
    first, last = end_points()
    left = jnp.where(first, jnp.where(meta[2] == 0, bath, below), left)
    right = jnp.where(last, jnp.where(meta[2] == 15, bath, above), right)
    return (right - left) * 0.5


def largest_turn(note):
    lane = iota((1, LANES), 1)
    first, second, second_last, last = (note[r : r + 1, :] for r in range(1, 5))
    below = jnp.where(lane == 0, first, pltpu.roll(jnp.broadcast_to(last, (8, LANES)), 1, 1)[0:1, :])
    above = jnp.where(lane == 15, last, pltpu.roll(jnp.broadcast_to(first, (8, LANES)), LANES - 1, 1)[0:1, :])
    at_first = jnp.abs(second - below) * 0.5 * note[5:6, :]
    at_last = jnp.abs(above - second_last) * 0.5 * note[6:7, :]
    here = jnp.where(lane < 16, jnp.maximum(at_first, at_last), 0.0)
    return jnp.maximum(jnp.max(here), jnp.max(jnp.where(lane == 0, note[0:1, :], 0.0)))


def block_counts(count):
    tile_block = iota((TILES, LANES), 0) // 4
    counts = jnp.zeros((TILES, LANES), i32)
    for b in range(8):
        counts = jnp.where(tile_block == b, count[b], counts)
    return counts.astype(f32)


def turn_kernel(edge, meta, count, group_at, note_ref, other_ref, x_hbm, bath_ref, wet_ref, refr_ref, halo_ref, sines, left_ref, right_ref, left_hbm, right_hbm, *rest):
    if edge:
        y_ref, rim_ref, *rest = rest
    else:
        y_ref, *rest = rest
    if edge:
        x_ref = x_hbm
    else:
        *rest, x_ref, sems = rest
        (copy,) = fetch(((rows_of(x_hbm, edge, meta), x_ref),), sems)
    speed, left_wide, right_wide = rest
    note = jnp.maximum(note_ref[...], other_ref[0:8, :])
    scale = 0.5 / (jnp.full((TILES, LANES), largest_turn(note), f32) + EPSILON)
    wet = wet_ref[...].astype(f32)
    speed[...] = full_gradient(meta, note, bath_ref[...]) * wet * scale * COS_HALF / block_counts(count)
    first, groups = part(edge, meta)
    if not edge:
        copy.wait()
    overflow = jnp.max(jnp.where(iota((1, LANES), 1) == 2, note[0:1, :], LOW)) > GROUPS * LANES

    def halo(wide, d, g, refs, tile):
        ref, side = refs
        most = TILES - 1 if wide else GROUPS - 1

        def eight(k):
            return jnp.broadcast_to(halo_ref[pl.ds(k * TILES + tile, 1), :], (8, LANES))

        def slots(group):
            lanes = pl.ds(pl.multiple_of(jnp.minimum(group, most) * LANES, LANES), LANES)
            return ref[pl.ds(pl.multiple_of(((first + g) * D_LOC + d) * 8, 8), 8), lanes]

        group = group_at[0, side * 64 + tile]
        values = jnp.where(eight(2 + side) == 1, slots(group), slots(group + 1))
        return gather(values, eight(side))

    def sweep(wide, block, carry):
        low = (left_wide if wide else left_ref, 0)
        high = (right_wide if wide else right_ref, 1)
        steps = count[block]
        for kmax in range(1, KMAX + 1):

            @pl.when(steps == kmax)
            def _():
                done = []
                for j in range(4):
                    tile = 4 * block + j
                    drive = speed[pl.ds(tile, 1), :]
                    sine = [
                        sines[pl.ds(k * TILES + tile, 1), :] for k in range(KMAX - kmax, FACES - (KMAX - kmax))
                    ]
                    for g in range(groups):
                        group = first + g
                        base = refr_ref[pl.ds(pl.multiple_of(group * 256 + tile * 8, 8), 8), :] * drive
                        cells = []
                        for c in range(KMAX - kmax, D_LOC + KMAX + kmax):
                            d = c % D_LOC
                            if c < KMAX:
                                cells.append(halo(wide, d, g, low, tile))
                            elif c < KMAX + D_LOC:
                                cells.append(x_ref[pl.ds(g * 8 * ROWS + tile * D_LOC + d, 8, stride=ROWS), :])
                            else:
                                cells.append(halo(wide, d, g, high, tile))
                        face = [base * v for v in sine]
                        plus = [jnp.maximum(v, 0.0) for v in face]
                        minus = [jnp.minimum(v, 0.0) for v in face]
                        for step in range(kmax):
                            n = len(cells) - 1
                            flux = [
                                plus[step + i] * cells[i] + minus[step + i] * cells[i + 1] for i in range(n)
                            ]
                            cells = [cells[i + 1] - (flux[i + 1] - flux[i]) for i in range(n - 1)]
                        done.append((g, tile, cells))
                    if j % (4 // groups) != 4 // groups - 1:
                        continue
                    for g, at_tile, cells in done:
                        for d in range(D_LOC):
                            y_ref[pl.ds(g * 8 * ROWS + at_tile * D_LOC + d, 8, stride=ROWS), :] = cells[d]
                    done = []

        return carry

    @pl.when(overflow)
    def _():
        for ref, more, whole in ((left_ref, left_hbm, left_wide), (right_ref, right_hbm, right_wide)):
            whole[:, : GROUPS * LANES] = ref[...]
            pltpu.sync_copy(more, whole.at[:, GROUPS * LANES :])
        lax.fori_loop(0, 8, functools.partial(sweep, True), 0)

    @pl.when(jnp.logical_not(overflow))
    def _():
        lax.fori_loop(0, 8, functools.partial(sweep, False), 0)

    if edge:
        for m in range(KMAX):
            row = jnp.where(meta[1] == 0, 7 - m, m)
            rim_ref[m * ROWS : (m + 1) * ROWS, :] = y_ref[pl.ds(pl.multiple_of(row * ROWS, ROWS), ROWS), :]


def shift_kernel(rim, meta, count, note_ref, other_ref, near_ref, far_ref, shift_ref, wave_ref, wet_ref, *rest):
    if rim:
        rim_ref, _, out_hbm, wets, out_ref, sems = rest
    else:
        out_hbm, wets, out_ref, sems = rest
    note = jnp.maximum(note_ref[0:1, :], other_ref[0:1, :])
    peak = jnp.max(jnp.where(iota((1, LANES), 1) == 1, note, LOW))
    wets[...] = wet_ref[...].astype(f32)
    scale = 0.5 / (jnp.full((8, LANES), peak, f32) + EPSILON)
    upper_rows = iota((8, LANES), 0) < D_LOC

    def spread(ref, first, second):
        return jnp.where(upper_rows, ref[pl.ds(first, 1), :], ref[pl.ds(second, 1), :])

    def one(lower, pair, carry):
        tile = 2 * pair
        offset = pl.multiple_of(pair * 8, 8)
        eights = pl.multiple_of(tile * 8, 8)
        drive = wave_ref[pl.ds(offset, 8), :] * scale
        forward = drive > 0.0
        mask_wet = spread(wets, tile, tile + 1)

        def coefficient(g):
            if g >= F_LOC:
                at = 8 + (g - F_LOC) * TILES + tile
                return spread(other_ref, at, at + 1)
            f = g if lower else F_LOC - 1 - g
            at = (f // 8) * 256 + f % 8 + eights
            return spread(shift_ref, at, at + 8)

        def cell(g):
            if g >= F_LOC:
                ref, row = rim_ref, g - F_LOC
            elif g < 16:
                ref, row = far_ref, (g if lower else 15 - g)
            else:
                ref, row = near_ref, (g - 16 if lower else 23 - g)
            return ref[pl.ds(row * ROWS + offset, 8), :]

        steps = count[pair // 2]
        for kmax in range(1, KMAX + 1):

            @pl.when(steps == kmax)
            def _():
                which = range(16 - kmax, F_LOC + kmax) if rim else range(16 + kmax)
                cells = [cell(g) for g in which]
                coefs = [coefficient(g) for g in which]
                face = [(coefs[i] + coefs[i + 1]) * drive for i in range(len(coefs) - 1)]
                for step in range(kmax):
                    n = len(cells)
                    used = face[step:] if rim else face
                    flux = [used[i] * jnp.where(forward, cells[i], cells[i + 1]) for i in range(n - 1)]
                    inner = [cells[i] - (flux[i] - flux[i - 1]) for i in range(1, n - 1)]
                    cells = inner if rim else [cells[0] - flux[0]] + inner
                count_out = 8 if rim else 16
                for i in range(count_out):
                    row = i if lower else count_out - 1 - i
                    out_ref[row, pl.ds(offset, 8), :] = cells[i] * mask_wet

        return carry

    first, groups = part(rim, meta)

    def departure(c):
        rows = pl.ds(pl.multiple_of(c * 32, 32), 32)
        freqs = pl.ds(first * 8, groups * 8)
        return pltpu.make_async_copy(out_ref.at[:, rows, :], out_hbm.at[freqs, rows, :], sems.at[c])

    def quarter(lower, c, carry):
        lax.fori_loop(4 * c, 4 * c + 4, functools.partial(one, lower), 0)
        departure(c).start()
        return carry

    @pl.when(meta[1] == 0)
    def _():
        lax.fori_loop(0, 4, functools.partial(quarter, True), 0)

    @pl.when(meta[1] == 1)
    def _():
        lax.fori_loop(0, 4, functools.partial(quarter, False), 0)

    for c in range(4):
        departure(c).wait()


SMEM = pl.BlockSpec(memory_space=pltpu.SMEM)
VMEM = pl.BlockSpec(memory_space=pltpu.VMEM)
ANY = pl.BlockSpec(memory_space=pl.ANY)
HBM = pl.BlockSpec(memory_space=pltpu.HBM)


def call(body, outs, in_specs, scratch, args, out_specs=None, aliases=None):
    return pl.pallas_call(
        body,
        out_shape=outs,
        in_specs=in_specs,
        out_specs=out_specs if out_specs is not None else [VMEM] * len(outs),
        scratch_shapes=scratch,
        input_output_aliases=aliases or {},
        compiler_params=pltpu.CompilerParams(vmem_limit_bytes=VMEM_LIMIT),
        cost_estimate=pl.CostEstimate(flops=0, bytes_accessed=0, transcendentals=0),
    )(*args)


def in_hbm(*arrays):
    return [pltpu.with_memory_space_constraint(a, pltpu.HBM) for a in arrays]


def shape(*dims):
    return jax.ShapeDtypeStruct(dims, f32)


def local(action, bathymetry, refraction, shifting, heading, slope_angle, wet_mask, substeps):
    pts = lax.axis_index(("pts_0", "pts_1"))
    dir_index, freq_index = lax.axis_index("dir"), lax.axis_index("freq")
    meta = jnp.stack([dir_index, freq_index, pts, pts]).astype(i32)
    table = jnp.asarray(angle_table())
    x = action.reshape(F_LOC, D_LOC, TILES, LANES).transpose(0, 2, 1, 3).reshape(F_LOC * ROWS, LANES)
    bath, head, slope, wet = (
        a.reshape(TILES, LANES) for a in (bathymetry, heading, slope_angle, wet_mask)
    )

    def by_eight(a):
        return a.reshape(3, 8, TILES, LANES).transpose(0, 2, 1, 3).reshape(3 * TILES * 8, LANES)

    refr, shift = by_eight(refraction), by_eight(shifting)
    count = lax.axis_size("dir")
    ring_up = [(i, (i + 1) % count) for i in range(count)]
    ring_down = [((i + 1) % count, i) for i in range(count)]
    swap = [(0, 1), (1, 0)]

    waves_of = [[shape(SIDE, GROUPS * LANES)] * 2, [shape(SIDE, (TILES - GROUPS) * LANES)] * 2]
    row = pltpu.VMEM((TILES, LANES), f32)
    row_int = pltpu.VMEM((TILES, LANES), i32)

    def exchange(up, down):
        return lax.ppermute(up, "dir", ring_up), lax.ppermute(down, "dir", ring_down)

    small = [row, row, row_int]
    coefs = pltpu.VMEM((3 * TILES * 8, LANES), f32)
    dma = pltpu.SemaphoreType.DMA
    packed = pltpu.VMEM((SIDE, (TILES + 1) * LANES), f32)
    wide = pltpu.VMEM((SIDE, TILES * LANES), f32)

    def pack(wave):
        vmem_x = pltpu.VMEM((F_LOC * ROWS, LANES), f32)
        both = pltpu.VMEM((2 * TILES, LANES), i32)
        return call(
            functools.partial(pack_kernel, wave),
            waves_of[wave] + ([pltpu.VMEM((8 * ROWS, LANES), f32)] if wave == 0 else []),
            [SMEM, SMEM] + [HBM] * 4,
            small
            + [packed, packed, dma((3,)), dma((3,)), dma((3,)), dma((3,)), dma((1,)), dma((1,))]
            + [both, both, pltpu.VMEM((8, LANES), i32), pltpu.SMEM((8, LANES), i32)]
            + [vmem_x],
            (meta, table, *in_hbm(bath, slope, wet, x)),
            out_specs=[ANY, ANY] + ([VMEM] if wave == 0 else []),
        )

    up, down, x_edge = pack(0)
    left, right = exchange(up, down)
    note, halo, groups_at, sines, waves, shift_rim = call(
        note_kernel,
        [
            shape(8, LANES),
            jax.ShapeDtypeStruct((4 * TILES, LANES), i32),
            jax.ShapeDtypeStruct((8, LANES), i32),
            shape(FACES * TILES, LANES),
            shape(ROWS, LANES),
            shape(KMAX * TILES, LANES),
        ],
        [SMEM] * 3 + [HBM] * 6,
        small
        + [row, coefs, coefs, dma((6,)), row, row]
        + [pltpu.VMEM((8, LANES), f32), pltpu.VMEM((16 * TILES, LANES), f32)],
        (meta, table, substeps, *in_hbm(bath, slope, wet, head, refr, shift)),
    )
    for axis in ("pts_0", "pts_1"):
        note = lax.pmax(note, axis)
    other = lax.ppermute(jnp.concatenate([note, shift_rim], axis=0), "freq", swap)

    def second_wave():
        return exchange(*pack(1))

    def no_wave():
        return tuple(call(lambda *refs: None, waves_of[1], [], [], (), out_specs=[ANY, ANY]))

    left_more, right_more = lax.cond(note[0, 2] > GROUPS * LANES, second_wave, no_wave)

    def turn(edge):
        groups = 1 if edge else 2
        outs = [shape(groups * 8 * ROWS, LANES)] + ([shape(KMAX * ROWS, LANES)] if edge else [])
        return call(
            functools.partial(turn_kernel, edge),
            outs,
            [SMEM] * 3 + [VMEM] * 2 + [VMEM if edge else HBM] + [VMEM] * 7 + [HBM] * 2,
            [row, wide, wide] + ([] if edge else [pltpu.VMEM((groups * 8 * ROWS, LANES), f32), dma((1,))]),
            (meta, substeps, groups_at, note, other, *([x_edge] if edge else in_hbm(x)), bath, wet, refr, halo, sines, left, right, *in_hbm(left_more, right_more)),
        )

    near, rim = turn(True)
    other_rim = lax.ppermute(rim, "freq", swap)
    (far,) = turn(False)

    def shifted_part(rim, more):
        groups = 1 if rim else 2
        (out,) = call(
            functools.partial(shift_kernel, rim),
            [shape(F_LOC, ROWS, LANES)],
            [SMEM] * 2 + [VMEM] * 7 + [VMEM, ANY][: len(more)],
            [row, pltpu.VMEM((groups * 8, ROWS, LANES), f32), dma((4,))],
            (meta, substeps, note, other, near, far, shift, waves, wet, *more),
            out_specs=[ANY],
            aliases={10: 0} if rim else None,
        )
        return out

    out = shifted_part(True, (other_rim, shifted_part(False, ())))
    return out.reshape(F_LOC, TILES, D_LOC, LANES).transpose(0, 2, 1, 3).reshape(F_LOC, D_LOC, TILES * LANES)


PTS = ("pts_0", "pts_1")


def solution(mesh):
    torus = Mesh(
        mesh.devices.reshape(8, 2, mesh.shape["dir"], mesh.shape["freq"]),
        ("pts_0", "pts_1", "dir", "freq"),
    )
    in_specs = (
        P("freq", "dir", PTS),
        P(PTS),
        P("freq", PTS),
        P("freq", PTS),
        P(PTS),
        P(PTS),
        P(PTS),
        P(PTS),
    )
    return jax.shard_map(local, mesh=torus, in_specs=in_specs, out_specs=P("freq", "dir", PTS), check_vma=False)
```
